512 devices in a mesh: rep: 4 (over y_hi, core), row: 8 (over z), col: 16 (over y_lo, x).
Axes of the slice: x: 4, y: 8 (y_hi: 2, y_lo: 4; y = y_hi * 4 + y_lo), z: 8, core: 2. Of those that a mesh axis runs over, the one named last changes fastest.
Arguments:
- acts: bfloat16 [512, 16384], P('rep', 'row'), may hold values from -12 to 12
- grad_out: bfloat16 [512, 49152], P('rep', 'col'), may hold values from -32 to 32
- weight_slab: bfloat16 [4, 16384, 12288], P('rep', 'row', 'col'), may hold values from -0.02734375 to 0.02734375
Outputs:
- input_grad: bfloat16 [512, 16384], P(('rep', 'col'), 'row')
- left_stats: float32 [1024, 16384], P(('rep', 'col'), 'row')
- right_stats: float32 [1024, 49152], P(('rep', 'row'), 'col')
The draws below stay inside these ranges and needn't reach their ends.
All inputs are finite; a program needn't handle non-finite values.
Results may differ from the reference program's by a relative error of at most 0.0047.
Values may be sent and summed in bfloat16 or wider, within the bound.
No kernel may reach another device: no remote copies, remote signals or barrier semaphores. Data moves between devices by JAX's collectives and lax.ppermute only.
A program may use at most 64 MiB of HBM per device.

```python
import math
import jax
import jax.numpy as jnp

D = 16384
FF = 49152
BLOCK = 1024
TOK = 128
TOKENS = 512
CQ = 768
N_REP = 4
N_COL = 16


def column_scales(key, count, rise):
    position = jnp.arange(count, dtype=jnp.float32) / count
    mean_square = (rise * rise - 1.0) / math.log(rise * rise)
    rough = jax.random.uniform(key, (1, count), jnp.float32, 0.7, 1.4)
    return rough * jnp.exp(math.log(rise) * position)[None, :] / math.sqrt(mean_square)


def draw_grad_out(key, part):
    key = jax.random.fold_in(key, 11)
    first, second, third = jax.random.split(key, 3)
    scales = jnp.exp(jax.random.uniform(first, (TOKENS, 1), jnp.float32, math.log(0.5), math.log(2.0)))
    values = jnp.clip(jax.random.normal(second, (TOKENS, FF), jnp.float32), -4.0, 4.0)
    columns = column_scales(third, FF, 3.0)
    return (scales * values * columns).astype(jnp.bfloat16)


def draw_acts(key, part):
    key = jax.random.fold_in(key, 23)
    second, third = jax.random.split(key)
    values = jnp.clip(jax.random.normal(second, (TOKENS, D), jnp.float32), -4.0, 4.0)
    columns = column_scales(third, D, 3.0)
    return (values * columns).astype(jnp.bfloat16)


def block_levels(own_key, dims, cuts, smallest, largest):
    def one(dim, shards_of):
        steps = jax.random.uniform(jax.random.fold_in(jax.random.fold_in(own_key, 6), dim), (shards_of,), jnp.float32, smallest / len(cuts), largest / len(cuts))
        return jnp.repeat(jnp.exp(steps), dims[dim] // shards_of).reshape((-1,) + (1,) * (len(dims) - dim - 1))

    factor_of = one(*cuts[0])
    for cut in cuts[1:]:
        factor_of = factor_of * one(*cut)
    return factor_of


def gaussian(own_key, extent, scale, limit, cuts=(), kind=jnp.bfloat16):
    level = block_levels(own_key, extent, cuts, -0.22, 0.18) if cuts else 1.0
    drawn = jax.random.normal(own_key, extent, jnp.float32) * scale * level
    return jnp.minimum(jnp.maximum(drawn, -limit), limit).astype(kind)


def setup_inputs(seed: int = 0) -> dict:
    arg_keys = jax.random.split(jax.random.key(seed), 4)
    acts = draw_acts(jax.random.fold_in(arg_keys[3], 71), 0)
    grad_out = draw_grad_out(jax.random.fold_in(arg_keys[3], 71), 0)
    weight_slab = gaussian(arg_keys[2], (N_REP, D, FF // N_REP), FF ** -0.5, 0.02734375, ((0, 4), (1, 8), (2, 16)))
    return {"acts": acts, "grad_out": grad_out, "weight_slab": weight_slab}


def reference(acts, grad_out, weight_slab):
    weight_t = weight_slab.reshape(N_REP, D, N_COL, CQ).transpose(2, 0, 3, 1).reshape(FF, D)
    input_grad = jnp.dot(grad_out, weight_t, preferred_element_type=jnp.float32).astype(jnp.bfloat16)
    grads = grad_out.reshape(N_REP, TOK, FF).astype(jnp.float32)
    inputs = acts.reshape(N_REP, TOK, D).astype(jnp.float32)
    left_kernel = (jnp.einsum("ptf,psf->pts", grads, grads) / FF).astype(jnp.bfloat16)
    right_kernel = (jnp.einsum("ptf,psf->pts", inputs, inputs) / D).astype(jnp.bfloat16)
    left_mix = jnp.einsum("pts,psd->ptd", left_kernel.astype(jnp.float32), inputs).astype(jnp.bfloat16)
    right_mix = jnp.einsum("pts,psf->ptf", right_kernel.astype(jnp.float32), grads).astype(jnp.bfloat16)
    left_stats = jnp.einsum("ptia,ptib->aib", inputs.reshape(N_REP, TOK, D // BLOCK, BLOCK),
                            left_mix.astype(jnp.float32).reshape(N_REP, TOK, D // BLOCK, BLOCK))
    left_stats = left_stats.reshape(BLOCK, D) / (N_REP * TOK)
    right_stats = jnp.einsum("ptia,ptib->aib", grads.reshape(N_REP, TOK, FF // BLOCK, BLOCK),
                             right_mix.astype(jnp.float32).reshape(N_REP, TOK, FF // BLOCK, BLOCK))
    right_stats = right_stats.reshape(BLOCK, FF) / (N_REP * TOK)
    return input_grad, left_stats, right_stats
```

```python
import functools

import jax
import jax.numpy as jnp
from jax import lax
from jax.experimental import pallas as pl
from jax.experimental.pallas import tpu as pltpu
from jax.sharding import Mesh, PartitionSpec as P

D = 16384
FF = 49152
BLOCK = 1024
TOKENS = 512
NT = (((1,), (1,)), ((), ()))
BF = jnp.bfloat16
F32 = jnp.float32


def stats_kernel(place, total_ref, data_ref, keep_ref, send_ref, *, share, stride, norm):
    rows = 4 * share
    kernel = (total_ref[...] / norm).astype(BF)
    data = data_ref[...]
    mix = jnp.dot(kernel, data, preferred_element_type=F32).astype(BF)
    row = lax.broadcasted_iota(jnp.int32, (rows, BLOCK), 0)
    unit = lax.broadcasted_iota(jnp.int32, (rows, BLOCK), 1)
    peer = row // share
    rep = ((place[0] ^ (peer & 1)) * 2) + (place[1] ^ (peer >> 1))
    wanted = (rep * stride + place[2]) * share + (row % share)
    pick = jnp.where(unit == wanted, 1.0, 0.0).astype(BF)
    picked = lax.dot_general(pick, data, NT, preferred_element_type=F32).astype(BF)
    out = jnp.dot(picked, mix, preferred_element_type=F32) * (1.0 / TOKENS)
    keep_ref[...] = out[: rows // 2]
    send_ref[...] = out[rows // 2 :]


def stats_rows(place, total, data, share, stride, norm):
    tokens, width = data.shape
    half = 2 * share
    shape = jax.ShapeDtypeStruct((half, width), F32)
    spec = pl.BlockSpec((half, BLOCK), lambda j, place: (0, j))
    return pl.pallas_call(
        functools.partial(stats_kernel, share=share, stride=stride, norm=norm),
        out_shape=(shape, shape),
        grid_spec=pltpu.PrefetchScalarGridSpec(
            num_scalar_prefetch=1,
            grid=(width // BLOCK,),
            in_specs=[
                pl.BlockSpec((tokens, tokens), lambda j, place: (0, 0)),
                pl.BlockSpec((tokens, BLOCK), lambda j, place: (0, j)),
            ],
            out_specs=[spec, spec],
        ),
        compiler_params=pltpu.CompilerParams(vmem_limit_bytes=24 * 1024 * 1024),
    )(place, total, data)


def body(acts, grad_out, weight_slab):
    weight = weight_slab[0]
    width = acts.shape[1]
    hidden = grad_out.shape[1]
    quarter = weight.shape[1]
    yh, core, row, yl, xx = (lax.axis_index(n) for n in ("yh", "core", "row", "yl", "x"))
    reps = ("yh", "core")

    def swap(value, dy, dc):
        perm = [(i, i ^ (2 * dy + dc)) for i in range(4)]
        return lax.ppermute(value, reps, perm)

    def piece(dy, dc):
        q = (yh ^ dy) * 2 + (core ^ dc)
        return lax.dynamic_slice_in_dim(grad_out, q * quarter, quarter, 1)

    from_y = swap(piece(1, 0), 1, 0)
    from_yc = swap(piece(1, 1), 1, 1)
    from_c = swap(piece(0, 1), 0, 1)
    own = piece(0, 0)

    left_part = lax.dot_general(grad_out, grad_out, NT, preferred_element_type=F32)
    right_part = lax.dot_general(acts, acts, NT, preferred_element_type=F32)
    left_all = lax.all_to_all(
        jnp.broadcast_to(left_part[None], (16,) + left_part.shape), ("yl", "x"), 0, 0, tiled=True
    )
    left_sum = jnp.sum(left_all, axis=0)
    right_sum = right_part
    for step in (1, 2, 4):
        right_sum = right_sum + lax.ppermute(right_sum, "row", [(i, i ^ step) for i in range(8)])

    def product(tokens):
        return lax.dot_general(tokens, weight, NT, preferred_element_type=F32)

    halves = []
    for near, far in ((own, from_c), (from_y, from_yc)):
        other = swap(product(far), 0, 1)
        both = (product(near) + other).astype(BF)
        both = both.reshape(4, 4, 8, width).transpose(1, 0, 2, 3)
        got = lax.all_to_all(both, "x", 0, 0, tiled=True)
        halves.append(jnp.sum(got.astype(F32), axis=0).astype(BF))
    first = jnp.where(yh == 0, halves[0], halves[1])
    second = jnp.where(yh == 0, halves[1], halves[0])
    chunks = jnp.concatenate([first, second], axis=0)
    got = lax.all_to_all(chunks, ("yh", "yl"), 0, 0, tiled=True)
    input_grad = jnp.sum(got.astype(F32), axis=0).astype(BF)

    def stats(total, data, share, stride, offset, norm):
        place = jnp.stack([yh, core, offset]).astype(jnp.int32)
        keep, send = stats_rows(place, total, data, share, stride, norm)
        both = keep + swap(send, 0, 1)
        far = swap(both[share:].astype(BF), 1, 0)
        return both[:share] + far.astype(F32)

    left_stats = stats(left_sum, acts, 16, 16, yl * 4 + xx, FF)
    right_stats = stats(right_sum, grad_out, 32, 8, row, D)
    return input_grad, left_stats, right_stats


def solution(mesh):
    split = Mesh(mesh.devices.reshape(2, 2, 8, 4, 4), ("yh", "core", "row", "yl", "x"))
    rep, col = ("yh", "core"), ("yl", "x")
    in_specs = (P(rep, "row"), P(rep, col), P(rep, "row", col))
    out_specs = (P(rep + col, "row"), P(rep + col, "row"), P(rep + ("row",), col))
    return jax.shard_map(body, mesh=split, in_specs=in_specs, out_specs=out_specs, check_vma=False)
```

```python
import functools

import jax
import jax.numpy as jnp
from jax import lax
from jax.experimental import pallas as pl
from jax.experimental.pallas import tpu as pltpu
from jax.sharding import Mesh, PartitionSpec as P

D = 16384
FF = 49152
BLOCK = 1024
TOKENS = 512
NT = (((1,), (1,)), ((), ()))
BF = jnp.bfloat16
F32 = jnp.float32
MB = 1024 * 1024


def params(mb):
    return pltpu.CompilerParams(vmem_limit_bytes=mb * MB)


def cost(flops, moved):
    return pl.CostEstimate(flops=flops, bytes_accessed=moved, transcendentals=0)


def prepare_kernel(place, acts_hbm, grads_hbm, own_ref, other_ref, direct_ref, share_ref, left_ref, right_ref, acts_ref, grads_ref, sems):
    quarter = own_ref.shape[1]
    rows = share_ref.shape[0]
    chunk = BLOCK

    def lanes(y, c):
        q = y * 2 + c
        return pl.ds(pl.multiple_of(q * quarter, quarter), quarter)

    turn = pl.ds(pl.multiple_of(place[2] * rows, rows), rows)
    yh, core = place[0], place[1]
    pieces = [
        (grads_hbm.at[turn, lanes(1 - yh, 1 - core)], share_ref),
        (grads_hbm.at[:, lanes(1 - yh, core)], direct_ref),
        (grads_hbm.at[:, lanes(yh, core)], own_ref),
        (grads_hbm.at[:, lanes(yh, 1 - core)], other_ref),
    ]
    copies = [pltpu.make_async_copy(grads_hbm, grads_ref, sems.at[0]), pltpu.make_async_copy(acts_hbm, acts_ref, sems.at[1])]
    copies += [pltpu.make_async_copy(s, d, sems.at[2 + i]) for i, (s, d) in enumerate(pieces)]
    for copy in copies:
        copy.start()
    copies[0].wait()
    left = lax.dot_general(grads_ref[turn, :], grads_ref[...], NT, preferred_element_type=F32)
    for i in range(left_ref.shape[0]):
        left_ref[i] = left
    copies[1].wait()
    acts = acts_ref[...]
    right = lax.dot_general(acts, acts, NT, preferred_element_type=F32).astype(BF)
    for i in range(right.shape[0] // rows):
        right_ref[:, i * 128 : i * 128 + 128] = right[i * rows : i * rows + rows]
    for copy in copies[2:]:
        copy.wait()


def prepare(place, acts, grads, cols, rows):
    tokens, hidden = grads.shape
    quarter = hidden // 4
    share = tokens // rows
    piece = jax.ShapeDtypeStruct((tokens, quarter), BF)
    return pl.pallas_call(
        prepare_kernel,
        out_shape=(
            piece,
            piece,
            piece,
            jax.ShapeDtypeStruct((share, quarter), BF),
            jax.ShapeDtypeStruct((cols, share, tokens), F32),
            jax.ShapeDtypeStruct((share, rows * tokens), BF),
        ),
        in_specs=[
            pl.BlockSpec(memory_space=pltpu.SMEM),
            pl.BlockSpec(memory_space=pltpu.HBM),
            pl.BlockSpec(memory_space=pltpu.HBM),
        ],
        out_specs=[pl.BlockSpec(memory_space=pltpu.VMEM)] * 6,
        scratch_shapes=[pltpu.VMEM(acts.shape, BF), pltpu.VMEM(grads.shape, BF), pltpu.SemaphoreType.DMA((6,))],
        compiler_params=params(56),
        cost_estimate=cost(2 * tokens * tokens * (hidden + acts.shape[1]), 3 * MB),
    )(place, acts, grads)


def pack_kernel(left_ref, right_ref, share_ref, out_ref):
    quarter = share_ref.shape[1]
    products = right_ref.shape[1]
    left = left_ref[0]
    for i in range(1, left_ref.shape[0]):
        left = left + left_ref[i]
    left = (left / FF).astype(BF)
    for z in range(out_ref.shape[0]):
        out_ref[z, :, :quarter] = share_ref[...]
        out_ref[z, :, quarter : quarter + products] = right_ref[...]
        out_ref[z, :, quarter + products :] = left


def pack(left, right, share, rows):
    width = share.shape[1] + right.shape[1] + left.shape[2]
    vmem = pl.BlockSpec(memory_space=pltpu.VMEM)
    return pl.pallas_call(
        pack_kernel,
        out_shape=jax.ShapeDtypeStruct((rows, share.shape[0], width), BF),
        in_specs=[vmem] * 3,
        out_specs=vmem,
        compiler_params=params(16),
        cost_estimate=cost(MB, MB),
    )(left, right, share)


def product_kernel(place, own_ref, other_ref, near_lo, near_hi, far_lo, far_hi, *rest):
    outs, low, high = rest[:4], rest[4], rest[5]
    own = own_ref[...]
    other = other_ref[...].reshape(own.shape)

    def dot(near, far):
        return lax.dot_general(own, near[...], NT, preferred_element_type=F32) + lax.dot_general(
            other, far[...], NT, preferred_element_type=F32
        )

    low[...] = dot(near_lo, far_lo)
    high[...] = dot(near_hi, far_hi)
    for r in range(4):
        for y in range(4):
            rows = pl.ds(pl.multiple_of((y * 4 + (place[4] ^ r)) * 8, 8), 8)
            pair = jnp.concatenate([low[rows, :], high[rows, :]], axis=0)
            outs[r][y * 16 : y * 16 + 16, :] = pair.astype(BF)


def product(place, own, other, weight, weight_far):
    count = own.shape[0]
    features, quarter = weight.shape
    half = features // 2
    step = 256
    steps = half // step
    low = pl.BlockSpec((step, quarter), lambda j, place: (j, 0))
    high = pl.BlockSpec((step, quarter), lambda j, place: (j + steps, 0))
    if other.ndim == 3:
        second = pl.BlockSpec(other.shape[:2] + (quarter,), lambda j, place: (0, 0, 0))
    else:
        second = pl.BlockSpec((count, quarter), lambda j, place: (0, 0))
    shape = jax.ShapeDtypeStruct((count // 2, half), BF)
    return pl.pallas_call(
        product_kernel,
        out_shape=(shape,) * 4,
        grid_spec=pltpu.PrefetchScalarGridSpec(
            num_scalar_prefetch=1,
            grid=(steps,),
            in_specs=[pl.BlockSpec((count, quarter), lambda j, place: (0, 0)), second, low, high, low, high],
            out_specs=[pl.BlockSpec((count // 2, step), lambda j, place: (0, j))] * 4,
            scratch_shapes=[pltpu.VMEM((count, step), F32)] * 2,
        ),
        compiler_params=params(16),
        cost_estimate=cost(4 * count * features * quarter, 7 * MB),
    )(place, own, other, weight, weight, weight_far, weight_far)


def x_sum_kernel(place, *refs):
    out_ref = refs[-1]

    def total(parts):
        value = parts[0][...].astype(F32)
        for part in parts[1:]:
            value = value + part[...].astype(F32)
        return value.astype(BF)

    out_ref[place[0]] = total(refs[:4])
    out_ref[1 - place[0]] = total(refs[4:8])


def x_sum(place, near, far):
    rows, width = near[0].shape
    vmem = pl.BlockSpec(memory_space=pltpu.VMEM)
    return pl.pallas_call(
        x_sum_kernel,
        out_shape=jax.ShapeDtypeStruct((2, rows, width), BF),
        in_specs=[pl.BlockSpec(memory_space=pltpu.SMEM)] + [vmem] * 8,
        out_specs=vmem,
        compiler_params=params(16),
        cost_estimate=cost(8 * rows * width, 2 * MB),
    )(place, *near, *far)


def y_sum_kernel(got_ref, out_ref):
    value = got_ref[0].astype(F32)
    for i in range(1, got_ref.shape[0]):
        value = value + got_ref[i].astype(F32)
    out_ref[...] = jnp.concatenate([value[:8], value[8:]], axis=1).astype(BF)


def y_sum(got):
    width = got.shape[2]
    return pl.pallas_call(
        y_sum_kernel,
        out_shape=jax.ShapeDtypeStruct((8, 2 * width), BF),
        in_specs=[pl.BlockSpec(memory_space=pltpu.VMEM)],
        out_specs=pl.BlockSpec(memory_space=pltpu.VMEM),
        compiler_params=params(16),
        cost_estimate=cost(128 * width, MB // 2),
    )(got)


def picker(place, offset, share, stride):
    shape = (4 * share, BLOCK)
    row = lax.broadcasted_iota(jnp.int32, shape, 0)
    unit = lax.broadcasted_iota(jnp.int32, shape, 1)
    peer = row // share
    rep = (place[0] ^ (peer & 1)) * 2 + (place[1] ^ (peer >> 1))
    wanted = (rep * stride + offset) * share + (row % share)
    return jnp.where(unit == wanted, 1.0, 0.0).astype(BF)


def stats_kernel(place, got_ref, acts_hbm, grads_hbm, keep_ref, send_ref, acts_ref, grads_ref, sems):
    hidden = grads_ref.shape[1]
    width = acts_ref.shape[1]
    tokens = acts_ref.shape[0]
    copies = []
    for j in range((hidden + width) // BLOCK):
        source, target, at = (grads_hbm, grads_ref, j) if j < hidden // BLOCK else (acts_hbm, acts_ref, j - hidden // BLOCK)
        lanes = slice(at * BLOCK, (at + 1) * BLOCK)
        copies.append(pltpu.make_async_copy(source.at[:, lanes], target.at[:, lanes], sems.at[j]))
        copies[-1].start()

    def rows(pick, token_kernel, data):
        mix = jnp.dot(token_kernel, data, preferred_element_type=F32).astype(BF)
        picked = lax.dot_general(pick, data, NT, preferred_element_type=F32).astype(BF)
        return jnp.dot(picked, mix, preferred_element_type=F32) * (1.0 / TOKENS)

    count, share, total = got_ref.shape
    products = slice(total - tokens - count * tokens, total - tokens)
    right = got_ref[0, :, products].astype(F32)
    for z in range(1, count):
        right = right + got_ref[z, :, products].astype(F32)
    right = jnp.concatenate([right[:, i * tokens : (i + 1) * tokens] for i in range(count)], axis=0)
    right = (right / D).astype(BF)
    pick = picker(place, place[2], 32, 8)
    for j in range(hidden // BLOCK):
        lanes = slice(j * BLOCK, (j + 1) * BLOCK)
        copies[j].wait()
        out = rows(pick, right, grads_ref[:, lanes])
        keep_ref[:, lanes] = out[:64]
        send_ref[:, lanes] = out[64:]
    left = jnp.concatenate([got_ref[z, :, total - tokens :] for z in range(count)], axis=0)
    pick = picker(place, place[3], 16, 16)
    for j in range(width // BLOCK):
        copies[hidden // BLOCK + j].wait()
        out = rows(pick, left, acts_ref[:, j * BLOCK : (j + 1) * BLOCK])
        for dy in range(2):
            at = slice(dy * 32 + j * 16, dy * 32 + j * 16 + 16)
            keep_ref[at, hidden:] = out[dy * 16 : dy * 16 + 16]
            send_ref[at, hidden:] = out[32 + dy * 16 : 32 + dy * 16 + 16]


def stats(place, got, acts, grads):
    shape = jax.ShapeDtypeStruct((64, grads.shape[1] + BLOCK), F32)
    vmem = pl.BlockSpec(memory_space=pltpu.VMEM)
    hbm = pl.BlockSpec(memory_space=pltpu.HBM)
    return pl.pallas_call(
        stats_kernel,
        out_shape=(shape, shape),
        in_specs=[pl.BlockSpec(memory_space=pltpu.SMEM), vmem, hbm, hbm],
        out_specs=[vmem, vmem],
        scratch_shapes=[
            pltpu.VMEM(acts.shape, BF),
            pltpu.VMEM(grads.shape, BF),
            pltpu.SemaphoreType.DMA(((acts.shape[1] + grads.shape[1]) // BLOCK,)),
        ],
        compiler_params=params(16),
        cost_estimate=cost(1000 * MB, 5 * MB),
    )(place, got, acts, grads)


def core_sum_kernel(keep_ref, got_ref, near_ref, far_ref):
    half = near_ref.shape[0]
    near_ref[...] = keep_ref[:half] + got_ref[:half]
    far_ref[...] = (keep_ref[half:] + got_ref[half:]).astype(BF)


def core_sum(keep, got):
    rows, width = keep.shape
    vmem = pl.BlockSpec(memory_space=pltpu.VMEM)
    return pl.pallas_call(
        core_sum_kernel,
        out_shape=(
            jax.ShapeDtypeStruct((rows // 2, width), F32),
            jax.ShapeDtypeStruct((rows // 2, width), BF),
        ),
        in_specs=[vmem, vmem],
        out_specs=[vmem, vmem],
        compiler_params=params(16),
        cost_estimate=cost(rows * width, 3 * MB),
    )(keep, got)


def last_sum_kernel(near_ref, far_ref, left_ref, right_ref):
    hidden = right_ref.shape[1]
    right_ref[...] = near_ref[:, :hidden] + far_ref[:, :hidden].astype(F32)
    for j in range(left_ref.shape[1] // BLOCK):
        rows = slice(j * 16, j * 16 + 16)
        left_ref[:, j * BLOCK : (j + 1) * BLOCK] = near_ref[rows, hidden:] + far_ref[rows, hidden:].astype(F32)


def last_sum(near, far, hidden, width):
    vmem = pl.BlockSpec(memory_space=pltpu.VMEM)
    return pl.pallas_call(
        last_sum_kernel,
        out_shape=(
            jax.ShapeDtypeStruct((16, width), F32),
            jax.ShapeDtypeStruct((32, hidden), F32),
        ),
        in_specs=[vmem, vmem],
        out_specs=[vmem, vmem],
        compiler_params=params(16),
        cost_estimate=cost(32 * 4096, 2 * MB),
    )(near, far)


def body(acts, grad_out, weight_slab):
    weight = weight_slab[0]
    width = acts.shape[1]
    hidden = grad_out.shape[1]
    yh, core, row, yl, xx = (lax.axis_index(n) for n in ("yh", "core", "row", "yl", "x"))
    place = jnp.stack([yh, core, row, yl * 4 + xx, xx]).astype(jnp.int32)

    def swap(value, axis):
        return lax.ppermute(value, axis, [(0, 1), (1, 0)])

    def to_x_peers(parts):
        return [parts[0]] + [
            lax.ppermute(parts[r], "x", [(i, i ^ r) for i in range(4)]) for r in (2, 1, 3)
        ]

    own, other, direct, share, left_part, right_part = prepare(place, acts, grad_out, 16, 8)
    share = swap(share, "yh")
    left_part, weight, direct = lax.optimization_barrier((left_part, weight, direct))
    left_rows = lax.all_to_all(left_part, ("yl", "x"), 0, 0, tiled=True)
    direct = swap(direct, "yh")
    weight_far = swap(weight, "core")

    packed = pack(left_rows, right_part, share, 8)
    got = lax.all_to_all(packed, "row", 0, 0, tiled=True)

    near = to_x_peers(product(place, own, other, weight, weight_far))

    keep, send = stats(place, got, acts, grad_out)
    near_rows, far_rows = core_sum(keep, swap(send, "core"))
    far_rows = swap(far_rows, "yh")

    far = to_x_peers(product(place, direct, got, weight, weight_far))
    chunks = x_sum(place, near, far)
    chunks = chunks.reshape(8, -1, chunks.shape[2])
    input_grad = y_sum(lax.all_to_all(chunks, ("yh", "yl"), 0, 0, tiled=True))

    left_stats, right_stats = last_sum(near_rows, far_rows, hidden, width)
    return input_grad, left_stats, right_stats


def solution(mesh):
    split = Mesh(mesh.devices.reshape(2, 2, 8, 4, 4), ("yh", "core", "row", "yl", "x"))
    rep, col = ("yh", "core"), ("yl", "x")
    in_specs = (P(rep, "row"), P(rep, col), P(rep, "row", col))
    out_specs = (P(rep + col, "row"), P(rep + col, "row"), P(rep + ("row",), col))
    return jax.shard_map(body, mesh=split, in_specs=in_specs, out_specs=out_specs, check_vma=False)
```

```python
import functools

import jax
import jax.numpy as jnp
from jax import lax
from jax.experimental import pallas as pl
from jax.experimental.pallas import tpu as pltpu
from jax.sharding import Mesh, PartitionSpec as P

D = 16384
FF = 49152
BLOCK = 1024
TOKENS = 512
NT = (((1,), (1,)), ((), ()))
BF = jnp.bfloat16
F32 = jnp.float32
MB = 1024 * 1024


def params(mb):
    return pltpu.CompilerParams(vmem_limit_bytes=mb * MB)


def cost(flops, moved):
    return pl.CostEstimate(flops=flops, bytes_accessed=moved, transcendentals=0)


def prepare_kernel(place, acts_hbm, grads_hbm, own_ref, other_ref, direct_ref, share_ref, left_ref, right_ref, acts_ref, grads_ref, sems):
    quarter = own_ref.shape[1]
    rows = share_ref.shape[0]
    chunk = BLOCK

    def lanes(y, c):
        q = y * 2 + c
        return pl.ds(pl.multiple_of(q * quarter, quarter), quarter)

    turn = pl.ds(pl.multiple_of(place[2] * rows, rows), rows)
    yh, core = place[0], place[1]
    pieces = [
        (grads_hbm.at[turn, lanes(1 - yh, 1 - core)], share_ref),
        (grads_hbm.at[:, lanes(1 - yh, core)], direct_ref),
        (grads_hbm.at[:, lanes(yh, core)], own_ref),
        (grads_hbm.at[:, lanes(yh, 1 - core)], other_ref),
    ]
    copies = [pltpu.make_async_copy(grads_hbm, grads_ref, sems.at[0]), pltpu.make_async_copy(acts_hbm, acts_ref, sems.at[1])]
    copies += [pltpu.make_async_copy(s, d, sems.at[2 + i]) for i, (s, d) in enumerate(pieces)]
    for copy in copies:
        copy.start()
    copies[0].wait()
    left = lax.dot_general(grads_ref[turn, :], grads_ref[...], NT, preferred_element_type=F32)
    for i in range(left_ref.shape[0]):
        left_ref[i] = left
    copies[1].wait()
    acts = acts_ref[...]
    right = lax.dot_general(acts, acts, NT, preferred_element_type=F32).astype(BF)
    for i in range(right.shape[0] // rows):
        right_ref[:, i * 128 : i * 128 + 128] = right[i * rows : i * rows + rows]
    for copy in copies[2:]:
        copy.wait()


def prepare(place, acts, grads, cols, rows):
    tokens, hidden = grads.shape
    quarter = hidden // 4
    share = tokens // rows
    piece = jax.ShapeDtypeStruct((tokens, quarter), BF)
    return pl.pallas_call(
        prepare_kernel,
        out_shape=(
            piece,
            piece,
            piece,
            jax.ShapeDtypeStruct((share, quarter), BF),
            jax.ShapeDtypeStruct((cols, share, tokens), F32),
            jax.ShapeDtypeStruct((share, rows * tokens), BF),
        ),
        in_specs=[
            pl.BlockSpec(memory_space=pltpu.SMEM),
            pl.BlockSpec(memory_space=pltpu.HBM),
            pl.BlockSpec(memory_space=pltpu.HBM),
        ],
        out_specs=[pl.BlockSpec(memory_space=pltpu.VMEM)] * 6,
        scratch_shapes=[pltpu.VMEM(acts.shape, BF), pltpu.VMEM(grads.shape, BF), pltpu.SemaphoreType.DMA((6,))],
        compiler_params=params(56),
        cost_estimate=cost(2 * tokens * tokens * (hidden + acts.shape[1]), 3 * MB),
    )(place, acts, grads)


def pack_kernel(left_ref, right_ref, share_ref, out_ref):
    quarter = share_ref.shape[1]
    products = right_ref.shape[1]
    left = left_ref[0]
    for i in range(1, left_ref.shape[0]):
        left = left + left_ref[i]
    left = (left / FF).astype(BF)
    for z in range(out_ref.shape[0]):
        out_ref[z, :, :quarter] = share_ref[...]
        out_ref[z, :, quarter : quarter + products] = right_ref[...]
        out_ref[z, :, quarter + products :] = left


def pack(left, right, share, rows):
    width = share.shape[1] + right.shape[1] + left.shape[2]
    vmem = pl.BlockSpec(memory_space=pltpu.VMEM)
    return pl.pallas_call(
        pack_kernel,
        out_shape=jax.ShapeDtypeStruct((rows, share.shape[0], width), BF),
        in_specs=[vmem] * 3,
        out_specs=vmem,
        compiler_params=params(16),
        cost_estimate=cost(MB, MB),
    )(left, right, share)


def product_kernel(place, own_ref, other_ref, near_lo, near_hi, far_lo, far_hi, *rest):
    outs, low, high = rest[:-2], rest[-2], rest[-1]
    own = own_ref[...]
    other = other_ref[...].reshape(own.shape)

    def dot(near, far):
        return lax.dot_general(own, near[...], NT, preferred_element_type=F32) + lax.dot_general(
            other, far[...], NT, preferred_element_type=F32
        )

    low[...] = dot(near_lo, far_lo)
    high[...] = dot(near_hi, far_hi)
    for r in range(4):
        for y in range(4):
            x = place[4] ^ r if len(outs) == 4 else r
            rows = pl.ds(pl.multiple_of((y * 4 + x) * 8, 8), 8)
            pair = jnp.concatenate([low[rows, :], high[rows, :]], axis=0).astype(BF)
            if len(outs) == 4:
                outs[r][y * 16 : y * 16 + 16, :] = pair
            else:
                outs[0][r, y * 16 : y * 16 + 16, :] = pair


def product(place, own, other, weight, weight_far, by_peer):
    count = own.shape[0]
    features, quarter = weight.shape
    half = features // 2
    step = 256
    steps = half // step
    low = pl.BlockSpec((step, quarter), lambda j, place: (j, 0))
    high = pl.BlockSpec((step, quarter), lambda j, place: (j + steps, 0))
    if other.ndim == 3:
        second = pl.BlockSpec(other.shape[:2] + (quarter,), lambda j, place: (0, 0, 0))
    else:
        second = pl.BlockSpec((count, quarter), lambda j, place: (0, 0))
    if by_peer:
        shape = (jax.ShapeDtypeStruct((count // 2, half), BF),) * 4
        out_specs = [pl.BlockSpec((count // 2, step), lambda j, place: (0, j))] * 4
    else:
        shape = jax.ShapeDtypeStruct((4, count // 2, half), BF)
        out_specs = pl.BlockSpec((4, count // 2, step), lambda j, place: (0, 0, j))
    return pl.pallas_call(
        product_kernel,
        out_shape=shape,
        grid_spec=pltpu.PrefetchScalarGridSpec(
            num_scalar_prefetch=1,
            grid=(steps,),
            in_specs=[pl.BlockSpec((count, quarter), lambda j, place: (0, 0)), second, low, high, low, high],
            out_specs=out_specs,
            scratch_shapes=[pltpu.VMEM((count, step), F32)] * 2,
        ),
        compiler_params=params(16),
        cost_estimate=cost(4 * count * features * quarter, 7 * MB),
    )(place, own, other, weight, weight, weight_far, weight_far)


def x_sum_kernel(place, own_ref, near1_ref, near2_ref, near3_ref, far_ref, out_ref):
    def total(parts):
        value = parts[0].astype(F32)
        for part in parts[1:]:
            value = value + part.astype(F32)
        return value.astype(BF)

    out_ref[place[0]] = total([own_ref[...], near1_ref[...], near2_ref[...], near3_ref[...]])
    out_ref[1 - place[0]] = total([far_ref[i] for i in range(far_ref.shape[0])])


def x_sum(place, near, far):
    rows, width = near[0].shape
    vmem = pl.BlockSpec(memory_space=pltpu.VMEM)
    return pl.pallas_call(
        x_sum_kernel,
        out_shape=jax.ShapeDtypeStruct((2, rows, width), BF),
        in_specs=[pl.BlockSpec(memory_space=pltpu.SMEM)] + [vmem] * 5,
        out_specs=vmem,
        compiler_params=params(16),
        cost_estimate=cost(8 * rows * width, 2 * MB),
    )(place, *near, far)


def y_sum_kernel(got_ref, out_ref):
    value = got_ref[0].astype(F32)
    for i in range(1, got_ref.shape[0]):
        value = value + got_ref[i].astype(F32)
    out_ref[...] = jnp.concatenate([value[:8], value[8:]], axis=1).astype(BF)


def y_sum(got):
    width = got.shape[2]
    return pl.pallas_call(
        y_sum_kernel,
        out_shape=jax.ShapeDtypeStruct((8, 2 * width), BF),
        in_specs=[pl.BlockSpec(memory_space=pltpu.VMEM)],
        out_specs=pl.BlockSpec(memory_space=pltpu.VMEM),
        compiler_params=params(16),
        cost_estimate=cost(128 * width, MB // 2),
    )(got)


def picker(place, offset, share, stride):
    shape = (4 * share, BLOCK)
    row = lax.broadcasted_iota(jnp.int32, shape, 0)
    unit = lax.broadcasted_iota(jnp.int32, shape, 1)
    peer = row // share
    rep = (place[0] ^ (peer & 1)) * 2 + (place[1] ^ (peer >> 1))
    wanted = (rep * stride + offset) * share + (row % share)
    return jnp.where(unit == wanted, 1.0, 0.0).astype(BF)


def stats_kernel(place, got_ref, acts_hbm, grads_hbm, keep_ref, send_ref, acts_ref, grads_ref, sems):
    hidden = grads_ref.shape[1]
    width = acts_ref.shape[1]
    tokens = acts_ref.shape[0]
    copies = []
    for j in range((hidden + width) // BLOCK):
        source, target, at = (grads_hbm, grads_ref, j) if j < hidden // BLOCK else (acts_hbm, acts_ref, j - hidden // BLOCK)
        lanes = slice(at * BLOCK, (at + 1) * BLOCK)
        copies.append(pltpu.make_async_copy(source.at[:, lanes], target.at[:, lanes], sems.at[j]))
        copies[-1].start()

    def rows(pick, token_kernel, data):
        mix = jnp.dot(token_kernel, data, preferred_element_type=F32).astype(BF)
        picked = lax.dot_general(pick, data, NT, preferred_element_type=F32).astype(BF)
        return jnp.dot(picked, mix, preferred_element_type=F32) * (1.0 / TOKENS)

    count, share, total = got_ref.shape
    products = slice(total - tokens - count * tokens, total - tokens)
    right = got_ref[0, :, products].astype(F32)
    for z in range(1, count):
        right = right + got_ref[z, :, products].astype(F32)
    right = jnp.concatenate([right[:, i * tokens : (i + 1) * tokens] for i in range(count)], axis=0)
    right = (right / D).astype(BF)
    pick = picker(place, place[2], 32, 8)
    for j in range(hidden // BLOCK):
        lanes = slice(j * BLOCK, (j + 1) * BLOCK)
        copies[j].wait()
        out = rows(pick, right, grads_ref[:, lanes])
        keep_ref[:, lanes] = out[:64]
        send_ref[:, lanes] = out[64:]
    left = jnp.concatenate([got_ref[z, :, total - tokens :] for z in range(count)], axis=0)
    pick = picker(place, place[3], 16, 16)
    for j in range(width // BLOCK):
        copies[hidden // BLOCK + j].wait()
        out = rows(pick, left, acts_ref[:, j * BLOCK : (j + 1) * BLOCK])
        for dy in range(2):
            at = slice(dy * 32 + j * 16, dy * 32 + j * 16 + 16)
            keep_ref[at, hidden:] = out[dy * 16 : dy * 16 + 16]
            send_ref[at, hidden:] = out[32 + dy * 16 : 32 + dy * 16 + 16]


def stats(place, got, acts, grads):
    shape = jax.ShapeDtypeStruct((64, grads.shape[1] + BLOCK), F32)
    vmem = pl.BlockSpec(memory_space=pltpu.VMEM)
    hbm = pl.BlockSpec(memory_space=pltpu.HBM)
    return pl.pallas_call(
        stats_kernel,
        out_shape=(shape, shape),
        in_specs=[pl.BlockSpec(memory_space=pltpu.SMEM), vmem, hbm, hbm],
        out_specs=[vmem, vmem],
        scratch_shapes=[
            pltpu.VMEM(acts.shape, BF),
            pltpu.VMEM(grads.shape, BF),
            pltpu.SemaphoreType.DMA(((acts.shape[1] + grads.shape[1]) // BLOCK,)),
        ],
        compiler_params=params(16),
        cost_estimate=cost(1000 * MB, 5 * MB),
    )(place, got, acts, grads)


def core_sum_kernel(keep_ref, got_ref, near_ref, far_ref):
    half = near_ref.shape[0]
    near_ref[...] = keep_ref[:half] + got_ref[:half]
    far_ref[...] = (keep_ref[half:] + got_ref[half:]).astype(BF)


def core_sum(keep, got):
    rows, width = keep.shape
    vmem = pl.BlockSpec(memory_space=pltpu.VMEM)
    return pl.pallas_call(
        core_sum_kernel,
        out_shape=(
            jax.ShapeDtypeStruct((rows // 2, width), F32),
            jax.ShapeDtypeStruct((rows // 2, width), BF),
        ),
        in_specs=[vmem, vmem],
        out_specs=[vmem, vmem],
        compiler_params=params(16),
        cost_estimate=cost(rows * width, 3 * MB),
    )(keep, got)


def last_sum_kernel(near_ref, far_ref, left_ref, right_ref):
    hidden = right_ref.shape[1]
    right_ref[...] = near_ref[:, :hidden] + far_ref[:, :hidden].astype(F32)
    for j in range(left_ref.shape[1] // BLOCK):
        rows = slice(j * 16, j * 16 + 16)
        left_ref[:, j * BLOCK : (j + 1) * BLOCK] = near_ref[rows, hidden:] + far_ref[rows, hidden:].astype(F32)


def last_sum(near, far, hidden, width):
    vmem = pl.BlockSpec(memory_space=pltpu.VMEM)
    return pl.pallas_call(
        last_sum_kernel,
        out_shape=(
            jax.ShapeDtypeStruct((16, width), F32),
            jax.ShapeDtypeStruct((32, hidden), F32),
        ),
        in_specs=[vmem, vmem],
        out_specs=[vmem, vmem],
        compiler_params=params(16),
        cost_estimate=cost(32 * 4096, 2 * MB),
    )(near, far)


def body(acts, grad_out, weight_slab):
    weight = weight_slab[0]
    width = acts.shape[1]
    hidden = grad_out.shape[1]
    yh, core, row, yl, xx = (lax.axis_index(n) for n in ("yh", "core", "row", "yl", "x"))
    place = jnp.stack([yh, core, row, yl * 4 + xx, xx]).astype(jnp.int32)

    def swap(value, axis):
        return lax.ppermute(value, axis, [(0, 1), (1, 0)])

    def to_x_peers(parts):
        return [parts[0]] + [
            lax.ppermute(parts[r], "x", [(i, i ^ r) for i in range(4)]) for r in (2, 1, 3)
        ]

    barrier = lax.optimization_barrier
    own, other, direct, share, left_part, right_part = prepare(place, acts, grad_out, 16, 8)
    share = swap(share, "yh")
    left_part, weight_sent, direct = barrier((left_part, weight, direct))
    left_rows = lax.all_to_all(left_part, ("yl", "x"), 0, 0, tiled=True)
    direct = swap(direct, "yh")
    weight_far = swap(weight_sent, "core")

    left_rows, share, weight_far = barrier((left_rows, share, weight_far))
    packed, own = barrier((pack(left_rows, right_part, share, 8), own))
    got = lax.all_to_all(packed, "row", 0, 0, tiled=True)
    near = to_x_peers(product(place, own, other, weight, weight_far, True))
    got, direct, near = barrier((got, direct, near))

    keep, send = stats(place, got, acts, grad_out)
    send, direct = barrier((send, direct))
    back = swap(send, "core")
    far = product(place, direct, got, weight, weight_far, False)
    back, far = barrier((back, far))
    near_rows, far_rows = core_sum(keep, back)
    far = lax.all_to_all(far, "x", 0, 0, tiled=True)
    far, near_rows, far_rows = barrier((far, near_rows, far_rows))
    far_rows = swap(far_rows, "yh")

    chunks = x_sum(place, near, far)
    chunks = chunks.reshape(8, -1, chunks.shape[2])
    input_grad = y_sum(lax.all_to_all(chunks, ("yh", "yl"), 0, 0, tiled=True))

    left_stats, right_stats = last_sum(near_rows, far_rows, hidden, width)
    return input_grad, left_stats, right_stats


def solution(mesh):
    split = Mesh(mesh.devices.reshape(2, 2, 8, 4, 4), ("yh", "core", "row", "yl", "x"))
    rep, col = ("yh", "core"), ("yl", "x")
    in_specs = (P(rep, "row"), P(rep, col), P(rep, "row", col))
    out_specs = (P(rep + col, "row"), P(rep + col, "row"), P(rep + ("row",), col))
    return jax.shard_map(body, mesh=split, in_specs=in_specs, out_specs=out_specs, check_vma=False)
```

```python
import functools

import jax
import jax.numpy as jnp
from jax import lax
from jax.experimental import pallas as pl
from jax.experimental.pallas import tpu as pltpu
from jax.sharding import Mesh, PartitionSpec as P

D = 16384
FF = 49152
BLOCK = 1024
TOKENS = 512
NT = (((1,), (1,)), ((), ()))
BF = jnp.bfloat16
F32 = jnp.float32
MB = 1024 * 1024


def params(mb):
    return pltpu.CompilerParams(vmem_limit_bytes=mb * MB)


def cost(flops, moved):
    return pl.CostEstimate(flops=flops, bytes_accessed=moved, transcendentals=0)


def prepare_kernel(place, acts_ref, grads_ref, left_ref, right_ref):
    rows = right_ref.shape[0]
    turn = pl.ds(pl.multiple_of(place[2] * rows, rows), rows)
    left = lax.dot_general(grads_ref[turn, :], grads_ref[...], NT, preferred_element_type=F32)
    for i in range(left_ref.shape[0]):
        left_ref[i] = left
    acts = acts_ref[...]
    right = lax.dot_general(acts, acts, NT, preferred_element_type=F32).astype(BF)
    for i in range(right.shape[0] // rows):
        right_ref[:, i * 128 : i * 128 + 128] = right[i * rows : i * rows + rows]


def prepare(place, acts, grads, cols, rows):
    tokens, hidden = grads.shape
    share = tokens // rows
    vmem = pl.BlockSpec(memory_space=pltpu.VMEM)
    return pl.pallas_call(
        prepare_kernel,
        out_shape=(
            jax.ShapeDtypeStruct((cols, share, tokens), F32),
            jax.ShapeDtypeStruct((share, rows * tokens), BF),
        ),
        in_specs=[pl.BlockSpec(memory_space=pltpu.SMEM), vmem, vmem],
        out_specs=[vmem] * 2,
        compiler_params=params(60),
        cost_estimate=cost(2 * tokens * tokens * (hidden + acts.shape[1]), 3 * MB),
    )(place, acts, grads)


def pack_kernel(left_ref, right_ref, share_ref, out_ref):
    quarter = share_ref.shape[1]
    products = right_ref.shape[1]
    left = left_ref[0]
    for i in range(1, left_ref.shape[0]):
        left = left + left_ref[i]
    left = (left / FF).astype(BF)
    for z in range(out_ref.shape[0]):
        out_ref[z, :, :quarter] = share_ref[...]
        out_ref[z, :, quarter : quarter + products] = right_ref[...]
        out_ref[z, :, quarter + products :] = left


def pack(left, right, share, rows):
    width = share.shape[1] + right.shape[1] + left.shape[2]
    vmem = pl.BlockSpec(memory_space=pltpu.VMEM)
    return pl.pallas_call(
        pack_kernel,
        out_shape=jax.ShapeDtypeStruct((rows, share.shape[0], width), BF),
        in_specs=[vmem] * 3,
        out_specs=vmem,
        compiler_params=params(60),
        cost_estimate=cost(MB, MB),
    )(left, right, share)


def product_kernel(place, tokens_ref, near_lo, near_hi, far_lo, far_hi, *rest):
    outs, low, high = rest[:-2], rest[-2], rest[-1]
    quarter = near_lo.shape[1]

    def piece(core):
        lanes = pl.ds(pl.multiple_of(core * quarter, quarter), quarter)
        if len(tokens_ref.shape) == 3:
            return tokens_ref[:, :, lanes].reshape(-1, quarter)
        return tokens_ref[:, lanes]

    own, other = piece(place[1]), piece(1 - place[1])

    def dot(near, far):
        return lax.dot_general(own, near[...], NT, preferred_element_type=F32) + lax.dot_general(
            other, far[...], NT, preferred_element_type=F32
        )

    low[...] = dot(near_lo, far_lo)
    high[...] = dot(near_hi, far_hi)
    for r in range(4):
        for y in range(4):
            x = place[4] ^ r if len(outs) == 4 else r
            rows = pl.ds(pl.multiple_of((y * 4 + x) * 8, 8), 8)
            pair = jnp.concatenate([low[rows, :], high[rows, :]], axis=0).astype(BF)
            if len(outs) == 4:
                outs[r][y * 16 : y * 16 + 16, :] = pair
            else:
                outs[0][r, y * 16 : y * 16 + 16, :] = pair


def product(place, tokens, weight, weight_far, by_peer):
    features, quarter = weight.shape
    half = features // 2
    step = 256
    steps = half // step
    low = pl.BlockSpec((step, quarter), lambda j, place: (j, 0))
    high = pl.BlockSpec((step, quarter), lambda j, place: (j + steps, 0))
    if tokens.ndim == 3:
        count = tokens.shape[0] * tokens.shape[1]
        token_spec = pl.BlockSpec(tokens.shape[:2] + (2 * quarter,), lambda j, place: (0, 0, 0))
    else:
        count = tokens.shape[0]
        token_spec = pl.BlockSpec((count, 2 * quarter), lambda j, place: (0, place[0]))
    if by_peer:
        shape = (jax.ShapeDtypeStruct((count // 2, half), BF),) * 4
        out_specs = [pl.BlockSpec((count // 2, step), lambda j, place: (0, j))] * 4
    else:
        shape = jax.ShapeDtypeStruct((4, count // 2, half), BF)
        out_specs = pl.BlockSpec((4, count // 2, step), lambda j, place: (0, 0, j))
    return pl.pallas_call(
        product_kernel,
        out_shape=shape,
        grid_spec=pltpu.PrefetchScalarGridSpec(
            num_scalar_prefetch=1,
            grid=(steps,),
            in_specs=[token_spec, low, high, low, high],
            out_specs=out_specs,
            scratch_shapes=[pltpu.VMEM((count, step), F32)] * 2,
        ),
        compiler_params=params(60),
        cost_estimate=cost(4 * count * features * quarter, 7 * MB),
    )(place, tokens, weight, weight, weight_far, weight_far)


def x_sum_kernel(place, own_ref, near1_ref, near2_ref, near3_ref, far_ref, out_ref):
    def total(parts):
        value = parts[0].astype(F32)
        for part in parts[1:]:
            value = value + part.astype(F32)
        return value.astype(BF)

    out_ref[place[0]] = total([own_ref[...], near1_ref[...], near2_ref[...], near3_ref[...]])
    out_ref[1 - place[0]] = total([far_ref[i] for i in range(far_ref.shape[0])])


def x_sum(place, near, far):
    rows, width = near[0].shape
    vmem = pl.BlockSpec(memory_space=pltpu.VMEM)
    return pl.pallas_call(
        x_sum_kernel,
        out_shape=jax.ShapeDtypeStruct((2, rows, width), BF),
        in_specs=[pl.BlockSpec(memory_space=pltpu.SMEM)] + [vmem] * 5,
        out_specs=vmem,
        compiler_params=params(60),
        cost_estimate=cost(8 * rows * width, 2 * MB),
    )(place, *near, far)


def y_sum_kernel(got_ref, out_ref):
    value = got_ref[0].astype(F32)
    for i in range(1, got_ref.shape[0]):
        value = value + got_ref[i].astype(F32)
    out_ref[...] = jnp.concatenate([value[:8], value[8:]], axis=1).astype(BF)


def y_sum(got):
    width = got.shape[2]
    return pl.pallas_call(
        y_sum_kernel,
        out_shape=jax.ShapeDtypeStruct((8, 2 * width), BF),
        in_specs=[pl.BlockSpec(memory_space=pltpu.VMEM)],
        out_specs=pl.BlockSpec(memory_space=pltpu.VMEM),
        compiler_params=params(60),
        cost_estimate=cost(128 * width, MB // 2),
    )(got)


def picker(place, offset, share, stride):
    shape = (4 * share, BLOCK)
    row = lax.broadcasted_iota(jnp.int32, shape, 0)
    unit = lax.broadcasted_iota(jnp.int32, shape, 1)
    peer = row // share
    rep = (place[0] ^ (peer & 1)) * 2 + (place[1] ^ (peer >> 1))
    wanted = (rep * stride + offset) * share + (row % share)
    return jnp.where(unit == wanted, 1.0, 0.0).astype(BF)


def stats_kernel(place, got_ref, acts_hbm, grads_hbm, keep_ref, send_ref, acts_ref, grads_ref, sems):
    hidden = grads_ref.shape[1]
    width = acts_ref.shape[1]
    tokens = acts_ref.shape[0]
    copies = []
    for j in range((hidden + width) // BLOCK):
        source, target, at = (grads_hbm, grads_ref, j) if j < hidden // BLOCK else (acts_hbm, acts_ref, j - hidden // BLOCK)
        lanes = slice(at * BLOCK, (at + 1) * BLOCK)
        copies.append(pltpu.make_async_copy(source.at[:, lanes], target.at[:, lanes], sems.at[j]))
        copies[-1].start()

    def rows(pick, token_kernel, data):
        mix = jnp.dot(token_kernel, data, preferred_element_type=F32).astype(BF)
        picked = lax.dot_general(pick, data, NT, preferred_element_type=F32).astype(BF)
        return jnp.dot(picked, mix, preferred_element_type=F32) * (1.0 / TOKENS)

    count, share, total = got_ref.shape
    products = slice(total - tokens - count * tokens, total - tokens)
    right = got_ref[0, :, products].astype(F32)
    for z in range(1, count):
        right = right + got_ref[z, :, products].astype(F32)
    right = jnp.concatenate([right[:, i * tokens : (i + 1) * tokens] for i in range(count)], axis=0)
    right = (right / D).astype(BF)
    pick = picker(place, place[2], 32, 8)
    for j in range(hidden // BLOCK):
        lanes = slice(j * BLOCK, (j + 1) * BLOCK)
        copies[j].wait()
        out = rows(pick, right, grads_ref[:, lanes])
        keep_ref[:, lanes] = out[:64]
        send_ref[:, lanes] = out[64:]
    left = jnp.concatenate([got_ref[z, :, total - tokens :] for z in range(count)], axis=0)
    pick = picker(place, place[3], 16, 16)
    for j in range(width // BLOCK):
        copies[hidden // BLOCK + j].wait()
        out = rows(pick, left, acts_ref[:, j * BLOCK : (j + 1) * BLOCK])
        for dy in range(2):
            at = slice(dy * 32 + j * 16, dy * 32 + j * 16 + 16)
            keep_ref[at, hidden:] = out[dy * 16 : dy * 16 + 16]
            send_ref[at, hidden:] = out[32 + dy * 16 : 32 + dy * 16 + 16]


def stats(place, got, acts, grads):
    shape = jax.ShapeDtypeStruct((64, grads.shape[1] + BLOCK), F32)
    vmem = pl.BlockSpec(memory_space=pltpu.VMEM)
    hbm = pl.BlockSpec(memory_space=pltpu.HBM)
    return pl.pallas_call(
        stats_kernel,
        out_shape=(shape, shape),
        in_specs=[pl.BlockSpec(memory_space=pltpu.SMEM), vmem, hbm, hbm],
        out_specs=[vmem, vmem],
        scratch_shapes=[
            pltpu.VMEM(acts.shape, BF),
            pltpu.VMEM(grads.shape, BF),
            pltpu.SemaphoreType.DMA(((acts.shape[1] + grads.shape[1]) // BLOCK,)),
        ],
        compiler_params=params(60),
        cost_estimate=cost(1000 * MB, 5 * MB),
    )(place, got, acts, grads)


def core_sum_kernel(keep_ref, got_ref, near_ref, far_ref):
    half = near_ref.shape[0]
    near_ref[...] = keep_ref[:half] + got_ref[:half]
    far_ref[...] = (keep_ref[half:] + got_ref[half:]).astype(BF)


def core_sum(keep, got):
    rows, width = keep.shape
    vmem = pl.BlockSpec(memory_space=pltpu.VMEM)
    return pl.pallas_call(
        core_sum_kernel,
        out_shape=(
            jax.ShapeDtypeStruct((rows // 2, width), F32),
            jax.ShapeDtypeStruct((rows // 2, width), BF),
        ),
        in_specs=[vmem, vmem],
        out_specs=[vmem, vmem],
        compiler_params=params(60),
        cost_estimate=cost(rows * width, 3 * MB),
    )(keep, got)


def last_sum_kernel(near_ref, far_ref, left_ref, right_ref):
    hidden = right_ref.shape[1]
    right_ref[...] = near_ref[:, :hidden] + far_ref[:, :hidden].astype(F32)
    for j in range(left_ref.shape[1] // BLOCK):
        rows = slice(j * 16, j * 16 + 16)
        left_ref[:, j * BLOCK : (j + 1) * BLOCK] = near_ref[rows, hidden:] + far_ref[rows, hidden:].astype(F32)


def last_sum(near, far, hidden, width):
    vmem = pl.BlockSpec(memory_space=pltpu.VMEM)
    return pl.pallas_call(
        last_sum_kernel,
        out_shape=(
            jax.ShapeDtypeStruct((16, width), F32),
            jax.ShapeDtypeStruct((32, hidden), F32),
        ),
        in_specs=[vmem, vmem],
        out_specs=[vmem, vmem],
        compiler_params=params(60),
        cost_estimate=cost(32 * 4096, 2 * MB),
    )(near, far)


def body(acts, grad_out, weight_slab):
    weight = weight_slab[0]
    width = acts.shape[1]
    hidden = grad_out.shape[1]
    yh, core, row, yl, xx = (lax.axis_index(n) for n in ("yh", "core", "row", "yl", "x"))
    place = jnp.stack([yh, core, row, yl * 4 + xx, xx]).astype(jnp.int32)

    def swap(value, axis):
        return lax.ppermute(value, axis, [(0, 1), (1, 0)])

    def to_x_peers(parts):
        return [parts[0]] + [
            lax.ppermute(parts[r], "x", [(i, i ^ r) for i in range(4)]) for r in (2, 1, 3)
        ]

    barrier = lax.optimization_barrier
    share = lax.dynamic_slice(grad_out, (row * 16, (1 - yh) * (hidden // 2)), (16, hidden // 2))
    share = swap(share, "yh")
    left_part, right_part = prepare(place, acts, grad_out, 16, 8)
    left_rows = lax.all_to_all(left_part, ("yl", "x"), 0, 0, tiled=True)
    weight_far = swap(weight, "core")

    left_rows, share, weight_far = barrier((left_rows, share, weight_far))
    packed, near_tokens = barrier((pack(left_rows, right_part, share, 8), grad_out))
    got = lax.all_to_all(packed, "row", 0, 0, tiled=True)
    near = to_x_peers(product(place, near_tokens, weight, weight_far, True))
    got, near = barrier((got, near))

    keep, send = stats(place, got, acts, grad_out)
    send, far_tokens = barrier((send, got))
    back = swap(send, "core")
    far = product(place, far_tokens, weight, weight_far, False)
    back, far = barrier((back, far))
    near_rows, far_rows = core_sum(keep, back)
    far, far_rows = barrier((far, far_rows))
    far_rows = swap(far_rows, "yh")
    far = lax.all_to_all(far, "x", 0, 0, tiled=True)

    chunks = x_sum(place, near, far)
    chunks = chunks.reshape(8, -1, chunks.shape[2])
    chunks, far_rows = barrier((chunks, far_rows))
    input_grad = y_sum(lax.all_to_all(chunks, ("yh", "yl"), 0, 0, tiled=True))

    left_stats, right_stats = last_sum(near_rows, far_rows, hidden, width)
    return input_grad, left_stats, right_stats


def solution(mesh):
    split = Mesh(mesh.devices.reshape(2, 2, 8, 4, 4), ("yh", "core", "row", "yl", "x"))
    rep, col = ("yh", "core"), ("yl", "x")
    in_specs = (P(rep, "row"), P(rep, col), P(rep, "row", col))
    out_specs = (P(rep + col, "row"), P(rep + col, "row"), P(rep + ("row",), col))
    return jax.shard_map(body, mesh=split, in_specs=in_specs, out_specs=out_specs, check_vma=False)
```

```python
import functools

import jax
import jax.numpy as jnp
from jax import lax
from jax.experimental import pallas as pl
from jax.experimental.pallas import tpu as pltpu
from jax.sharding import Mesh, PartitionSpec as P

D = 16384
FF = 49152
BLOCK = 1024
TOKENS = 512
NT = (((1,), (1,)), ((), ()))
BF = jnp.bfloat16
F32 = jnp.float32
MB = 1024 * 1024


def params(mb):
    return pltpu.CompilerParams(vmem_limit_bytes=mb * MB)


def cost(flops, moved):
    return pl.CostEstimate(flops=flops, bytes_accessed=moved, transcendentals=0)


def prepare_kernel(place, acts_ref, grads_ref, left_ref, right_ref):
    rows = right_ref.shape[0]
    turn = pl.ds(pl.multiple_of(place[2] * rows, rows), rows)
    left = lax.dot_general(grads_ref[turn, :], grads_ref[...], NT, preferred_element_type=F32)
    for i in range(left_ref.shape[0]):
        left_ref[i] = left
    acts = acts_ref[...]
    right = lax.dot_general(acts, acts, NT, preferred_element_type=F32).astype(BF)
    for i in range(right.shape[0] // rows):
        right_ref[:, i * 128 : i * 128 + 128] = right[i * rows : i * rows + rows]


def prepare(place, acts, grads, cols, rows):
    tokens, hidden = grads.shape
    share = tokens // rows
    vmem = pl.BlockSpec(memory_space=pltpu.VMEM)
    return pl.pallas_call(
        prepare_kernel,
        out_shape=(
            jax.ShapeDtypeStruct((cols, share, tokens), F32),
            jax.ShapeDtypeStruct((share, rows * tokens), BF),
        ),
        in_specs=[pl.BlockSpec(memory_space=pltpu.SMEM), vmem, vmem],
        out_specs=[vmem] * 2,
        compiler_params=params(60),
        cost_estimate=cost(2 * tokens * tokens * (hidden + acts.shape[1]), 3 * MB),
    )(place, acts, grads)


def pack_kernel(left_ref, right_ref, share_ref, out_ref):
    quarter = share_ref.shape[1]
    products = right_ref.shape[1]
    left = left_ref[0]
    for i in range(1, left_ref.shape[0]):
        left = left + left_ref[i]
    left = (left / FF).astype(BF)
    for z in range(out_ref.shape[0]):
        out_ref[z, :, :quarter] = share_ref[...]
        out_ref[z, :, quarter : quarter + products] = right_ref[...]
        out_ref[z, :, quarter + products :] = left


def pack(left, right, share, rows):
    width = share.shape[1] + right.shape[1] + left.shape[2]
    vmem = pl.BlockSpec(memory_space=pltpu.VMEM)
    return pl.pallas_call(
        pack_kernel,
        out_shape=jax.ShapeDtypeStruct((rows, share.shape[0], width), BF),
        in_specs=[vmem] * 3,
        out_specs=vmem,
        compiler_params=params(60),
        cost_estimate=cost(MB, MB),
    )(left, right, share)


def product_kernel(place, tokens_ref, near_lo, near_hi, far_lo, far_hi, *rest):
    outs, low, high = rest[:-2], rest[-2], rest[-1]
    quarter = near_lo.shape[1]

    def piece(core):
        lanes = pl.ds(pl.multiple_of(core * quarter, quarter), quarter)
        if len(tokens_ref.shape) == 3:
            return tokens_ref[:, :, lanes].reshape(-1, quarter)
        return tokens_ref[:, lanes]

    own, other = piece(place[1]), piece(1 - place[1])

    def dot(near, far):
        return lax.dot_general(own, near[...], NT, preferred_element_type=F32) + lax.dot_general(
            other, far[...], NT, preferred_element_type=F32
        )

    low[...] = dot(near_lo, far_lo)
    high[...] = dot(near_hi, far_hi)
    for r in range(4):
        for y in range(4):
            x = (place[3] & 3) ^ r if len(outs) == 4 else r
            rows = pl.ds(pl.multiple_of((y * 4 + x) * 8, 8), 8)
            pair = jnp.concatenate([low[rows, :], high[rows, :]], axis=0).astype(BF)
            if len(outs) == 4:
                outs[r][y * 16 : y * 16 + 16, :] = pair
            else:
                outs[0][r, y * 16 : y * 16 + 16, :] = pair


def product(place, tokens, weight, weight_far, by_peer):
    features, quarter = weight.shape
    half = features // 2
    step = 256
    steps = half // step
    low = pl.BlockSpec((step, quarter), lambda j, place: (j, 0))
    high = pl.BlockSpec((step, quarter), lambda j, place: (j + steps, 0))
    if tokens.ndim == 3:
        count = tokens.shape[0] * tokens.shape[1]
        token_spec = pl.BlockSpec(tokens.shape[:2] + (2 * quarter,), lambda j, place: (0, 0, 0))
    else:
        count = tokens.shape[0]
        token_spec = pl.BlockSpec((count, 2 * quarter), lambda j, place: (0, place[0]))
    if by_peer:
        shape = (jax.ShapeDtypeStruct((count // 2, half), BF),) * 4
        out_specs = [pl.BlockSpec((count // 2, step), lambda j, place: (0, j))] * 4
    else:
        shape = jax.ShapeDtypeStruct((4, count // 2, half), BF)
        out_specs = pl.BlockSpec((4, count // 2, step), lambda j, place: (0, 0, j))
    return pl.pallas_call(
        product_kernel,
        out_shape=shape,
        grid_spec=pltpu.PrefetchScalarGridSpec(
            num_scalar_prefetch=1,
            grid=(steps,),
            in_specs=[token_spec, low, high, low, high],
            out_specs=out_specs,
            scratch_shapes=[pltpu.VMEM((count, step), F32)] * 2,
        ),
        compiler_params=params(16),
        cost_estimate=cost(4 * count * features * quarter, 7 * MB),
    )(place, tokens, weight, weight, weight_far, weight_far)


def x_sum_kernel(place, own_ref, near1_ref, near2_ref, near3_ref, far_ref, out_ref):
    def total(parts):
        value = parts[0].astype(F32)
        for part in parts[1:]:
            value = value + part.astype(F32)
        return value.astype(BF)

    out_ref[place[0]] = total([own_ref[...], near1_ref[...], near2_ref[...], near3_ref[...]])
    out_ref[1 - place[0]] = total([far_ref[i] for i in range(far_ref.shape[0])])


def x_sum(place, near, far):
    rows, width = near[0].shape
    vmem = pl.BlockSpec(memory_space=pltpu.VMEM)
    return pl.pallas_call(
        x_sum_kernel,
        out_shape=jax.ShapeDtypeStruct((2, rows, width), BF),
        in_specs=[pl.BlockSpec(memory_space=pltpu.SMEM)] + [vmem] * 5,
        out_specs=vmem,
        compiler_params=params(60),
        cost_estimate=cost(8 * rows * width, 2 * MB),
    )(place, *near, far)


def y_sum_kernel(got_ref, out_ref):
    value = got_ref[0].astype(F32)
    for i in range(1, got_ref.shape[0]):
        value = value + got_ref[i].astype(F32)
    out_ref[...] = jnp.concatenate([value[:8], value[8:]], axis=1).astype(BF)


def y_sum(got):
    width = got.shape[2]
    return pl.pallas_call(
        y_sum_kernel,
        out_shape=jax.ShapeDtypeStruct((8, 2 * width), BF),
        in_specs=[pl.BlockSpec(memory_space=pltpu.VMEM)],
        out_specs=pl.BlockSpec(memory_space=pltpu.VMEM),
        compiler_params=params(16),
        cost_estimate=cost(128 * width, MB // 2),
    )(got)


def picker(place, offset, share, stride):
    shape = (4 * share, BLOCK)
    row = lax.broadcasted_iota(jnp.int32, shape, 0)
    unit = lax.broadcasted_iota(jnp.int32, shape, 1)
    peer = row // share
    rep = (place[0] ^ (peer & 1)) * 2 + (place[1] ^ (peer >> 1))
    wanted = (rep * stride + offset) * share + (row % share)
    return jnp.where(unit == wanted, 1.0, 0.0).astype(BF)


def stats_kernel(place, got_ref, acts_hbm, grads_hbm, keep_ref, send_ref, acts_ref, grads_ref, sems):
    hidden = grads_ref.shape[1]
    width = acts_ref.shape[1]
    tokens = acts_ref.shape[0]
    copies = []
    for j in range((hidden + width) // BLOCK):
        source, target, at = (grads_hbm, grads_ref, j) if j < hidden // BLOCK else (acts_hbm, acts_ref, j - hidden // BLOCK)
        lanes = slice(at * BLOCK, (at + 1) * BLOCK)
        copies.append(pltpu.make_async_copy(source.at[:, lanes], target.at[:, lanes], sems.at[j]))
        copies[-1].start()

    def rows(pick, token_kernel, data):
        mix = jnp.dot(token_kernel, data, preferred_element_type=F32).astype(BF)
        picked = lax.dot_general(pick, data, NT, preferred_element_type=F32).astype(BF)
        return jnp.dot(picked, mix, preferred_element_type=F32) * (1.0 / TOKENS)

    count, share, total = got_ref.shape
    products = slice(total - tokens - count * tokens, total - tokens)
    right = got_ref[0, :, products].astype(F32)
    for z in range(1, count):
        right = right + got_ref[z, :, products].astype(F32)
    right = jnp.concatenate([right[:, i * tokens : (i + 1) * tokens] for i in range(count)], axis=0)
    right = (right / D).astype(BF)
    pick = picker(place, place[2], 32, 8)
    for j in range(hidden // BLOCK):
        lanes = slice(j * BLOCK, (j + 1) * BLOCK)
        copies[j].wait()
        out = rows(pick, right, grads_ref[:, lanes])
        keep_ref[:, lanes] = out[:64]
        send_ref[:, lanes] = out[64:]
    left = jnp.concatenate([got_ref[z, :, total - tokens :] for z in range(count)], axis=0)
    pick = picker(place, place[3], 16, 16)
    for j in range(width // BLOCK):
        copies[hidden // BLOCK + j].wait()
        out = rows(pick, left, acts_ref[:, j * BLOCK : (j + 1) * BLOCK])
        for dy in range(2):
            at = slice(dy * 32 + j * 16, dy * 32 + j * 16 + 16)
            keep_ref[at, hidden:] = out[dy * 16 : dy * 16 + 16]
            send_ref[at, hidden:] = out[32 + dy * 16 : 32 + dy * 16 + 16]


def stats(place, got, acts, grads):
    shape = jax.ShapeDtypeStruct((64, grads.shape[1] + BLOCK), F32)
    vmem = pl.BlockSpec(memory_space=pltpu.VMEM)
    hbm = pl.BlockSpec(memory_space=pltpu.HBM)
    return pl.pallas_call(
        stats_kernel,
        out_shape=(shape, shape),
        in_specs=[pl.BlockSpec(memory_space=pltpu.SMEM), vmem, hbm, hbm],
        out_specs=[vmem, vmem],
        scratch_shapes=[
            pltpu.VMEM(acts.shape, BF),
            pltpu.VMEM(grads.shape, BF),
            pltpu.SemaphoreType.DMA(((acts.shape[1] + grads.shape[1]) // BLOCK,)),
        ],
        compiler_params=params(16),
        cost_estimate=cost(1000 * MB, 5 * MB),
    )(place, got, acts, grads)


def core_sum_kernel(keep_ref, got_ref, near_ref, far_ref):
    half = near_ref.shape[0]
    near_ref[...] = keep_ref[:half] + got_ref[:half]
    far_ref[...] = (keep_ref[half:] + got_ref[half:]).astype(BF)


def core_sum(keep, got):
    rows, width = keep.shape
    vmem = pl.BlockSpec(memory_space=pltpu.VMEM)
    return pl.pallas_call(
        core_sum_kernel,
        out_shape=(
            jax.ShapeDtypeStruct((rows // 2, width), F32),
            jax.ShapeDtypeStruct((rows // 2, width), BF),
        ),
        in_specs=[vmem, vmem],
        out_specs=[vmem, vmem],
        compiler_params=params(16),
        cost_estimate=cost(rows * width, 3 * MB),
    )(keep, got)


def last_sum_kernel(near_ref, far_ref, left_ref, right_ref):
    hidden = right_ref.shape[1]
    right_ref[...] = near_ref[:, :hidden] + far_ref[:, :hidden].astype(F32)
    for j in range(left_ref.shape[1] // BLOCK):
        rows = slice(j * 16, j * 16 + 16)
        left_ref[:, j * BLOCK : (j + 1) * BLOCK] = near_ref[rows, hidden:] + far_ref[rows, hidden:].astype(F32)


def last_sum(near, far, hidden, width):
    vmem = pl.BlockSpec(memory_space=pltpu.VMEM)
    return pl.pallas_call(
        last_sum_kernel,
        out_shape=(
            jax.ShapeDtypeStruct((16, width), F32),
            jax.ShapeDtypeStruct((32, hidden), F32),
        ),
        in_specs=[vmem, vmem],
        out_specs=[vmem, vmem],
        compiler_params=params(16),
        cost_estimate=cost(32 * 4096, 2 * MB),
    )(near, far)


def body(acts, grad_out, weight_slab):
    weight = weight_slab[0]
    width = acts.shape[1]
    hidden = grad_out.shape[1]
    yh, core, row, yl, xx = (lax.axis_index(n) for n in ("yh", "core", "row", "yl", "x"))
    place = jnp.stack([yh, core, row, yl * 4 + xx]).astype(jnp.int32)

    def swap(value, axis):
        return lax.ppermute(value, axis, [(0, 1), (1, 0)])

    def to_x_peers(parts):
        return [parts[0]] + [
            lax.ppermute(parts[r], "x", [(i, i ^ r) for i in range(4)]) for r in (2, 1, 3)
        ]

    barrier = lax.optimization_barrier
    share = lax.dynamic_slice(grad_out, (row * 16, (1 - yh) * (hidden // 2)), (16, hidden // 2))
    share = swap(share, "yh")
    left_part, right_part = prepare(place, acts, grad_out, 16, 8)
    left_part, share = barrier((left_part, share))
    left_rows = lax.all_to_all(left_part, ("yl", "x"), 0, 0, tiled=True)
    weight_far = swap(weight, "core")

    left_rows, share, weight_far = barrier((left_rows, share, weight_far))
    packed, near_tokens = barrier((pack(left_rows, right_part, share, 8), grad_out))
    got = lax.all_to_all(packed, "row", 0, 0, tiled=True)
    near = to_x_peers(product(place, near_tokens, weight, weight_far, True))
    got, near[0], near[1], near[2] = barrier((got, near[0], near[1], near[2]))

    keep, send = stats(place, got, acts, grad_out)
    near_rows, far_rows = core_sum(keep, swap(send, "core"))
    far_tokens, far_rows = barrier((got, far_rows))
    far_rows = swap(far_rows, "yh")
    far = product(place, far_tokens, weight, weight_far, False)
    far = lax.all_to_all(far, "x", 0, 0, tiled=True)

    chunks = x_sum(place, near, far)
    chunks = chunks.reshape(8, -1, chunks.shape[2])
    chunks, far_rows = barrier((chunks, far_rows))
    input_grad = y_sum(lax.all_to_all(chunks, ("yh", "yl"), 0, 0, tiled=True))

    left_stats, right_stats = last_sum(near_rows, far_rows, hidden, width)
    return input_grad, left_stats, right_stats


def solution(mesh):
    split = Mesh(mesh.devices.reshape(2, 2, 8, 4, 4), ("yh", "core", "row", "yl", "x"))
    rep, col = ("yh", "core"), ("yl", "x")
    in_specs = (P(rep, "row"), P(rep, col), P(rep, "row", col))
    out_specs = (P(rep + col, "row"), P(rep + col, "row"), P(rep + ("row",), col))
    return jax.shard_map(body, mesh=split, in_specs=in_specs, out_specs=out_specs, check_vma=False)
```

```python
import functools

import jax
import jax.numpy as jnp
from jax import lax
from jax.experimental import pallas as pl
from jax.experimental.pallas import tpu as pltpu
from jax.sharding import Mesh, PartitionSpec as P

D = 16384
FF = 49152
BLOCK = 1024
TOKENS = 512
NT = (((1,), (1,)), ((), ()))
BF = jnp.bfloat16
F32 = jnp.float32
MB = 1024 * 1024


def params(mb):
    return pltpu.CompilerParams(vmem_limit_bytes=mb * MB)


def cost(flops, moved):
    return pl.CostEstimate(flops=flops, bytes_accessed=moved, transcendentals=0)


def prepare_kernel(acts_ref, grads_ref, sum_ref, send_ref):
    for i, ref in enumerate((grads_ref, acts_ref)):
        data = ref[...]
        value = lax.dot_general(data, data, NT, preferred_element_type=F32)
        sum_ref[i] = value
        send_ref[i] = value.astype(BF)


def prepare(acts, grads):
    tokens = grads.shape[0]
    vmem = pl.BlockSpec(memory_space=pltpu.VMEM)
    return pl.pallas_call(
        prepare_kernel,
        out_shape=(jax.ShapeDtypeStruct((2, tokens, tokens), F32), jax.ShapeDtypeStruct((2, tokens, tokens), BF)),
        in_specs=[vmem, vmem],
        out_specs=[vmem] * 2,
        compiler_params=params(16),
        cost_estimate=cost(2 * tokens * tokens * (grads.shape[1] + acts.shape[1]), 3 * MB),
    )(acts, grads)


def product_kernel(place, tokens_ref, near_lo, near_hi, far_lo, far_hi, *rest):
    out_ref, low, high = rest[-3:]
    quarter = near_lo.shape[1]

    def piece(core):
        lanes = pl.ds(pl.multiple_of(core * quarter, quarter), quarter)
        if len(tokens_ref.shape) == 3:
            return tokens_ref[:, :, lanes].reshape(-1, quarter)
        return tokens_ref[:, lanes]

    own, other = piece(place[1]), piece(1 - place[1])

    def dot(near, far):
        return lax.dot_general(own, near[...], NT, preferred_element_type=F32) + lax.dot_general(
            other, far[...], NT, preferred_element_type=F32
        )

    low[...] = dot(near_lo, far_lo)
    high[...] = dot(near_hi, far_hi)
    for x in range(4):
        for y in range(4):
            rows = slice((y * 4 + x) * 8, (y * 4 + x) * 8 + 8)
            pair = jnp.concatenate([low[rows, :], high[rows, :]], axis=0).astype(BF)
            out_ref[x, y * 16 : y * 16 + 16, :] = pair


def product(place, tokens, weight, weight_far, first=None):
    features, quarter = weight.shape
    half = features // 2
    step = 256
    steps = half // step
    low = pl.BlockSpec((step, quarter), lambda j, place: (j, 0))
    high = pl.BlockSpec((step, quarter), lambda j, place: (j + steps, 0))
    if tokens.ndim == 3:
        count = tokens.shape[0] * tokens.shape[1]
        token_spec = pl.BlockSpec(tokens.shape[:2] + (2 * quarter,), lambda j, place: (0, 0, 0))
    else:
        count = tokens.shape[0]
        token_spec = pl.BlockSpec((count, 2 * quarter), lambda j, place: (0, place[0]))
    in_specs = [token_spec, low, high, low, high]
    args = (place, tokens, weight, weight, weight_far, weight_far)
    part = 0
    aliases = {}
    if first is not None:
        in_specs.append(pl.BlockSpec(memory_space=pl.ANY))
        args += (first,)
        part = 1
        aliases = {6: 0}
    return pl.pallas_call(
        product_kernel,
        out_shape=jax.ShapeDtypeStruct((4, count, half), BF),
        grid_spec=pltpu.PrefetchScalarGridSpec(
            num_scalar_prefetch=1,
            grid=(steps,),
            in_specs=in_specs,
            out_specs=pl.BlockSpec((4, count // 2, step), lambda j, place: (0, part, j)),
            scratch_shapes=[pltpu.VMEM((count, step), F32)] * 2,
        ),
        input_output_aliases=aliases,
        compiler_params=params(60),
        cost_estimate=cost(4 * count * features * quarter, 7 * MB),
    )(*args)


def x_sum_kernel(place, got_ref, out_ref):
    rows = out_ref.shape[1]
    for part in range(2):
        value = got_ref[0, part * rows : part * rows + rows, :].astype(F32)
        for i in range(1, got_ref.shape[0]):
            value = value + got_ref[i, part * rows : part * rows + rows, :].astype(F32)
        out_ref[(1 - place[0]) if part else place[0]] = value.astype(BF)


def x_sum(place, got):
    _, rows, width = got.shape
    vmem = pl.BlockSpec(memory_space=pltpu.VMEM)
    return pl.pallas_call(
        x_sum_kernel,
        out_shape=jax.ShapeDtypeStruct((2, rows // 2, width), BF),
        in_specs=[pl.BlockSpec(memory_space=pltpu.SMEM), vmem],
        out_specs=vmem,
        compiler_params=params(16),
        cost_estimate=cost(8 * rows * width, 2 * MB),
    )(place, got)


def y_sum_kernel(got_ref, out_ref):
    value = got_ref[0].astype(F32)
    for i in range(1, got_ref.shape[0]):
        value = value + got_ref[i].astype(F32)
    out_ref[...] = jnp.concatenate([value[:8], value[8:]], axis=1).astype(BF)


def y_sum(got):
    width = got.shape[2]
    return pl.pallas_call(
        y_sum_kernel,
        out_shape=jax.ShapeDtypeStruct((8, 2 * width), BF),
        in_specs=[pl.BlockSpec(memory_space=pltpu.VMEM)],
        out_specs=pl.BlockSpec(memory_space=pltpu.VMEM),
        compiler_params=params(16),
        cost_estimate=cost(128 * width, MB // 2),
    )(got)


def picker(place, offset, share, stride):
    shape = (4 * share, BLOCK)
    row = lax.broadcasted_iota(jnp.int32, shape, 0)
    unit = lax.broadcasted_iota(jnp.int32, shape, 1)
    peer = row // share
    rep = (place[0] ^ (peer & 1)) * 2 + (place[1] ^ (peer >> 1))
    wanted = (rep * stride + offset) * share + (row % share)
    return jnp.where(unit == wanted, 1.0, 0.0).astype(BF)


def stats_kernel(place, left_ref, right_ref, acts_hbm, grads_hbm, keep_ref, send_ref, acts_ref, grads_ref, sems):
    hidden = grads_ref.shape[1]
    width = acts_ref.shape[1]
    copies = []
    for j in range((hidden + width) // BLOCK):
        source, target, at = (grads_hbm, grads_ref, j) if j < hidden // BLOCK else (acts_hbm, acts_ref, j - hidden // BLOCK)
        lanes = slice(at * BLOCK, (at + 1) * BLOCK)
        copies.append(pltpu.make_async_copy(source.at[:, lanes], target.at[:, lanes], sems.at[j]))
        copies[-1].start()

    def rows(pick, token_kernel, data):
        mix = jnp.dot(token_kernel, data, preferred_element_type=F32).astype(BF)
        picked = lax.dot_general(pick, data, NT, preferred_element_type=F32).astype(BF)
        return jnp.dot(picked, mix, preferred_element_type=F32) * (1.0 / TOKENS)

    right = (right_ref[...] / D).astype(BF)
    pick = picker(place, place[2], 32, 8)
    for j in range(hidden // BLOCK):
        lanes = slice(j * BLOCK, (j + 1) * BLOCK)
        copies[j].wait()
        out = rows(pick, right, grads_ref[:, lanes])
        keep_ref[:, lanes] = out[:64]
        send_ref[:, lanes] = out[64:]
    left = (left_ref[...] / FF).astype(BF)
    pick = picker(place, place[3], 16, 16)
    for j in range(width // BLOCK):
        copies[hidden // BLOCK + j].wait()
        out = rows(pick, left, acts_ref[:, j * BLOCK : (j + 1) * BLOCK])
        for dy in range(2):
            at = slice(dy * 32 + j * 16, dy * 32 + j * 16 + 16)
            keep_ref[at, hidden:] = out[dy * 16 : dy * 16 + 16]
            send_ref[at, hidden:] = out[32 + dy * 16 : 32 + dy * 16 + 16]


def stats(place, left, right, acts, grads):
    shape = jax.ShapeDtypeStruct((64, grads.shape[1] + BLOCK), F32)
    vmem = pl.BlockSpec(memory_space=pltpu.VMEM)
    hbm = pl.BlockSpec(memory_space=pltpu.HBM)
    return pl.pallas_call(
        stats_kernel,
        out_shape=(shape, shape),
        in_specs=[pl.BlockSpec(memory_space=pltpu.SMEM), vmem, vmem, hbm, hbm],
        out_specs=[vmem, vmem],
        scratch_shapes=[
            pltpu.VMEM(acts.shape, BF),
            pltpu.VMEM(grads.shape, BF),
            pltpu.SemaphoreType.DMA(((acts.shape[1] + grads.shape[1]) // BLOCK,)),
        ],
        compiler_params=params(16),
        cost_estimate=cost(1000 * MB, 5 * MB),
    )(place, left, right, acts, grads)


def core_sum_kernel(keep_ref, got_ref, near_ref, far_ref):
    half = near_ref.shape[0]
    near_ref[...] = keep_ref[:half] + got_ref[:half]
    far_ref[...] = (keep_ref[half:] + got_ref[half:]).astype(BF)


def core_sum(keep, got):
    rows, width = keep.shape
    vmem = pl.BlockSpec(memory_space=pltpu.VMEM)
    return pl.pallas_call(
        core_sum_kernel,
        out_shape=(
            jax.ShapeDtypeStruct((rows // 2, width), F32),
            jax.ShapeDtypeStruct((rows // 2, width), BF),
        ),
        in_specs=[vmem, vmem],
        out_specs=[vmem, vmem],
        compiler_params=params(16),
        cost_estimate=cost(rows * width, 3 * MB),
    )(keep, got)


def last_sum_kernel(near_ref, far_ref, left_ref, right_ref):
    hidden = right_ref.shape[1]
    right_ref[...] = near_ref[:, :hidden] + far_ref[:, :hidden].astype(F32)
    for j in range(left_ref.shape[1] // BLOCK):
        rows = slice(j * 16, j * 16 + 16)
        left_ref[:, j * BLOCK : (j + 1) * BLOCK] = near_ref[rows, hidden:] + far_ref[rows, hidden:].astype(F32)


def last_sum(near, far, hidden, width):
    vmem = pl.BlockSpec(memory_space=pltpu.VMEM)
    return pl.pallas_call(
        last_sum_kernel,
        out_shape=(
            jax.ShapeDtypeStruct((16, width), F32),
            jax.ShapeDtypeStruct((32, hidden), F32),
        ),
        in_specs=[vmem, vmem],
        out_specs=[vmem, vmem],
        compiler_params=params(16),
        cost_estimate=cost(32 * 4096, 2 * MB),
    )(near, far)


def body(acts, grad_out, weight_slab):
    weight = weight_slab[0]
    width = acts.shape[1]
    hidden = grad_out.shape[1]
    yh, core, row, yl, xx = (lax.axis_index(n) for n in ("yh", "core", "row", "yl", "x"))
    place = jnp.stack([yh, core, row, yl * 4 + xx]).astype(jnp.int32)

    def swap(value, axis):
        return lax.ppermute(value, axis, [(0, 1), (1, 0)])

    def across(value, dz, dy, dx):
        perm = [(i, i ^ (dz * 16 + dy * 4 + dx)) for i in range(128)]
        return lax.ppermute(value, ("row", "yl", "x"), perm)

    barrier = lax.optimization_barrier
    share = lax.dynamic_slice(grad_out, (row * 16, (1 - yh) * (hidden // 2)), (16, hidden // 2))
    share, acts_in = barrier((share, acts))
    share = swap(share, "yh")
    weight_far = swap(weight, "core")

    total, send = prepare(acts_in, grad_out)
    total = total + across(send, 1, 0, 1).astype(F32)
    total = total + across(total.astype(BF), 2, 0, 3).astype(F32)
    total = total + across(total.astype(BF), 7, 1, 0).astype(F32)
    left, right = total[0], total[1]
    left = left + across(left.astype(BF), 0, 2, 0).astype(F32)

    share = jnp.broadcast_to(share[None], (8,) + share.shape)
    share, near_tokens = barrier((share, grad_out))
    far_tokens = lax.all_to_all(share, "row", 0, 0, tiled=True)
    near = product(place, near_tokens, weight, weight_far)
    both = product(place, far_tokens, weight, weight_far, near)

    left, right, both = barrier((left, right, both))
    got = lax.all_to_all(both, "x", 0, 0, tiled=True)
    keep, send = stats(place, left, right, acts, grad_out)
    near_rows, far_rows = core_sum(keep, swap(send, "core"))
    got, near_rows = barrier((got, near_rows))
    far_rows = swap(far_rows, "yh")

    chunks = x_sum(place, got)
    chunks = chunks.reshape(8, -1, chunks.shape[2])
    input_grad = y_sum(lax.all_to_all(chunks, ("yh", "yl"), 0, 0, tiled=True))

    left_stats, right_stats = last_sum(near_rows, far_rows, hidden, width)
    return input_grad, left_stats, right_stats


def solution(mesh):
    split = Mesh(mesh.devices.reshape(2, 2, 8, 4, 4), ("yh", "core", "row", "yl", "x"))
    rep, col = ("yh", "core"), ("yl", "x")
    in_specs = (P(rep, "row"), P(rep, col), P(rep, "row", col))
    out_specs = (P(rep + col, "row"), P(rep + col, "row"), P(rep + ("row",), col))
    return jax.shard_map(body, mesh=split, in_specs=in_specs, out_specs=out_specs, check_vma=False)
```

```python
import functools

import jax
import jax.numpy as jnp
from jax import lax
from jax.experimental import pallas as pl
from jax.experimental.pallas import tpu as pltpu
from jax.sharding import Mesh, PartitionSpec as P

D = 16384
FF = 49152
BLOCK = 1024
TOKENS = 512
NT = (((1,), (1,)), ((), ()))
BF = jnp.bfloat16
F32 = jnp.float32
MB = 1024 * 1024


def params(mb):
    return pltpu.CompilerParams(vmem_limit_bytes=mb * MB)


def cost(flops, moved):
    return pl.CostEstimate(flops=flops, bytes_accessed=moved, transcendentals=0)


def prepare_kernel(acts_ref, grads_ref, sum_ref, send_ref):
    for i, ref in enumerate((grads_ref, acts_ref)):
        data = ref[...]
        value = lax.dot_general(data, data, NT, preferred_element_type=F32)
        sum_ref[i] = value
        send_ref[i] = value.astype(BF)


def prepare(acts, grads):
    tokens = grads.shape[0]
    vmem = pl.BlockSpec(memory_space=pltpu.VMEM)
    return pl.pallas_call(
        prepare_kernel,
        out_shape=(jax.ShapeDtypeStruct((2, tokens, tokens), F32), jax.ShapeDtypeStruct((2, tokens, tokens), BF)),
        in_specs=[vmem, vmem],
        out_specs=[vmem] * 2,
        compiler_params=params(16),
        cost_estimate=cost(2 * tokens * tokens * (grads.shape[1] + acts.shape[1]), 3 * MB),
    )(acts, grads)


def product_kernel(place, tokens_ref, near_lo, near_hi, far_lo, far_hi, *rest):
    out_ref, low, high = rest[-3:]
    quarter = near_lo.shape[1]

    def piece(core):
        lanes = pl.ds(pl.multiple_of(core * quarter, quarter), quarter)
        if len(tokens_ref.shape) == 3:
            return tokens_ref[:, :, lanes].reshape(-1, quarter)
        return tokens_ref[:, lanes]

    own, other = piece(place[1]), piece(1 - place[1])

    def dot(near, far):
        return lax.dot_general(own, near[...], NT, preferred_element_type=F32) + lax.dot_general(
            other, far[...], NT, preferred_element_type=F32
        )

    low[...] = dot(near_lo, far_lo)
    high[...] = dot(near_hi, far_hi)
    for x in range(4):
        for y in range(4):
            rows = slice((y * 4 + x) * 8, (y * 4 + x) * 8 + 8)
            pair = jnp.concatenate([low[rows, :], high[rows, :]], axis=0).astype(BF)
            out_ref[x, y * 16 : y * 16 + 16, :] = pair


def product(place, tokens, weight, weight_far, first=None):
    features, quarter = weight.shape
    half = features // 2
    step = 256
    steps = half // step
    low = pl.BlockSpec((step, quarter), lambda j, place: (j, 0))
    high = pl.BlockSpec((step, quarter), lambda j, place: (j + steps, 0))
    if tokens.ndim == 3:
        count = tokens.shape[0] * tokens.shape[1]
        token_spec = pl.BlockSpec(tokens.shape[:2] + (2 * quarter,), lambda j, place: (0, 0, 0))
    else:
        count = tokens.shape[0]
        token_spec = pl.BlockSpec((count, 2 * quarter), lambda j, place: (0, place[0]))
    in_specs = [token_spec, low, high, low, high]
    args = (place, tokens, weight, weight, weight_far, weight_far)
    part = 0
    aliases = {}
    if first is not None:
        in_specs.append(pl.BlockSpec(memory_space=pl.ANY))
        args += (first,)
        part = 1
        aliases = {6: 0}
    return pl.pallas_call(
        product_kernel,
        out_shape=jax.ShapeDtypeStruct((4, count, half), BF),
        grid_spec=pltpu.PrefetchScalarGridSpec(
            num_scalar_prefetch=1,
            grid=(steps,),
            in_specs=in_specs,
            out_specs=pl.BlockSpec((4, count // 2, step), lambda j, place: (0, part, j)),
            scratch_shapes=[pltpu.VMEM((count, step), F32)] * 2,
        ),
        input_output_aliases=aliases,
        compiler_params=params(60),
        cost_estimate=cost(4 * count * features * quarter, 7 * MB),
    )(*args)


def x_sum_kernel(place, got_ref, out_ref):
    rows = out_ref.shape[1]
    for part in range(2):
        value = got_ref[0, part * rows : part * rows + rows, :].astype(F32)
        for i in range(1, got_ref.shape[0]):
            value = value + got_ref[i, part * rows : part * rows + rows, :].astype(F32)
        out_ref[(1 - place[0]) if part else place[0]] = value.astype(BF)


def x_sum(place, got):
    _, rows, width = got.shape
    vmem = pl.BlockSpec(memory_space=pltpu.VMEM)
    return pl.pallas_call(
        x_sum_kernel,
        out_shape=jax.ShapeDtypeStruct((2, rows // 2, width), BF),
        in_specs=[pl.BlockSpec(memory_space=pltpu.SMEM), vmem],
        out_specs=vmem,
        compiler_params=params(16),
        cost_estimate=cost(8 * rows * width, 2 * MB),
    )(place, got)


def y_sum_kernel(got_ref, out_ref):
    value = got_ref[0].astype(F32)
    for i in range(1, got_ref.shape[0]):
        value = value + got_ref[i].astype(F32)
    out_ref[...] = jnp.concatenate([value[:8], value[8:]], axis=1).astype(BF)


def y_sum(got):
    width = got.shape[2]
    return pl.pallas_call(
        y_sum_kernel,
        out_shape=jax.ShapeDtypeStruct((8, 2 * width), BF),
        in_specs=[pl.BlockSpec(memory_space=pltpu.VMEM)],
        out_specs=pl.BlockSpec(memory_space=pltpu.VMEM),
        compiler_params=params(16),
        cost_estimate=cost(128 * width, MB // 2),
    )(got)


def picker(place, offset, share, stride):
    shape = (4 * share, BLOCK)
    row = lax.broadcasted_iota(jnp.int32, shape, 0)
    unit = lax.broadcasted_iota(jnp.int32, shape, 1)
    peer = row // share
    rep = (place[0] ^ (peer & 1)) * 2 + (place[1] ^ (peer >> 1))
    wanted = (rep * stride + offset) * share + (row % share)
    return jnp.where(unit == wanted, 1.0, 0.0).astype(BF)


def stats_kernel(place, left_ref, right_ref, acts_hbm, grads_hbm, keep_ref, send_ref, acts_ref, grads_ref, sems):
    hidden = grads_ref.shape[1]
    width = acts_ref.shape[1]
    copies = []
    for j in range((hidden + width) // BLOCK):
        source, target, at = (grads_hbm, grads_ref, j) if j < hidden // BLOCK else (acts_hbm, acts_ref, j - hidden // BLOCK)
        lanes = slice(at * BLOCK, (at + 1) * BLOCK)
        copies.append(pltpu.make_async_copy(source.at[:, lanes], target.at[:, lanes], sems.at[j]))
        copies[-1].start()

    def rows(pick, token_kernel, data):
        mix = jnp.dot(token_kernel, data, preferred_element_type=F32).astype(BF)
        picked = lax.dot_general(pick, data, NT, preferred_element_type=F32).astype(BF)
        return jnp.dot(picked, mix, preferred_element_type=F32) * (1.0 / TOKENS)

    right = (right_ref[...] / D).astype(BF)
    pick = picker(place, place[2], 32, 8)
    for j in range(hidden // BLOCK):
        lanes = slice(j * BLOCK, (j + 1) * BLOCK)
        copies[j].wait()
        out = rows(pick, right, grads_ref[:, lanes])
        keep_ref[:, lanes] = out[:64]
        send_ref[:, lanes] = out[64:]
    left = (left_ref[...] / FF).astype(BF)
    pick = picker(place, place[3], 16, 16)
    for j in range(width // BLOCK):
        copies[hidden // BLOCK + j].wait()
        out = rows(pick, left, acts_ref[:, j * BLOCK : (j + 1) * BLOCK])
        for dy in range(2):
            at = slice(dy * 32 + j * 16, dy * 32 + j * 16 + 16)
            keep_ref[at, hidden:] = out[dy * 16 : dy * 16 + 16]
            send_ref[at, hidden:] = out[32 + dy * 16 : 32 + dy * 16 + 16]


def stats(place, left, right, acts, grads):
    shape = jax.ShapeDtypeStruct((64, grads.shape[1] + BLOCK), F32)
    vmem = pl.BlockSpec(memory_space=pltpu.VMEM)
    hbm = pl.BlockSpec(memory_space=pltpu.HBM)
    return pl.pallas_call(
        stats_kernel,
        out_shape=(shape, shape),
        in_specs=[pl.BlockSpec(memory_space=pltpu.SMEM), vmem, vmem, hbm, hbm],
        out_specs=[vmem, vmem],
        scratch_shapes=[
            pltpu.VMEM(acts.shape, BF),
            pltpu.VMEM(grads.shape, BF),
            pltpu.SemaphoreType.DMA(((acts.shape[1] + grads.shape[1]) // BLOCK,)),
        ],
        compiler_params=params(16),
        cost_estimate=cost(1000 * MB, 5 * MB),
    )(place, left, right, acts, grads)


def core_sum_kernel(keep_ref, got_ref, near_ref, far_ref):
    half = near_ref.shape[0]
    near_ref[...] = keep_ref[:half] + got_ref[:half]
    far_ref[...] = (keep_ref[half:] + got_ref[half:]).astype(BF)


def core_sum(keep, got):
    rows, width = keep.shape
    vmem = pl.BlockSpec(memory_space=pltpu.VMEM)
    return pl.pallas_call(
        core_sum_kernel,
        out_shape=(
            jax.ShapeDtypeStruct((rows // 2, width), F32),
            jax.ShapeDtypeStruct((rows // 2, width), BF),
        ),
        in_specs=[vmem, vmem],
        out_specs=[vmem, vmem],
        compiler_params=params(16),
        cost_estimate=cost(rows * width, 3 * MB),
    )(keep, got)


def last_sum_kernel(near_ref, far_ref, left_ref, right_ref):
    hidden = right_ref.shape[1]
    right_ref[...] = near_ref[:, :hidden] + far_ref[:, :hidden].astype(F32)
    for j in range(left_ref.shape[1] // BLOCK):
        rows = slice(j * 16, j * 16 + 16)
        left_ref[:, j * BLOCK : (j + 1) * BLOCK] = near_ref[rows, hidden:] + far_ref[rows, hidden:].astype(F32)


def last_sum(near, far, hidden, width):
    vmem = pl.BlockSpec(memory_space=pltpu.VMEM)
    return pl.pallas_call(
        last_sum_kernel,
        out_shape=(
            jax.ShapeDtypeStruct((16, width), F32),
            jax.ShapeDtypeStruct((32, hidden), F32),
        ),
        in_specs=[vmem, vmem],
        out_specs=[vmem, vmem],
        compiler_params=params(16),
        cost_estimate=cost(32 * 4096, 2 * MB),
    )(near, far)


def body(acts, grad_out, weight_slab):
    weight = weight_slab[0]
    width = acts.shape[1]
    hidden = grad_out.shape[1]
    yh, core, row, yl, xx = (lax.axis_index(n) for n in ("yh", "core", "row", "yl", "x"))
    place = jnp.stack([yh, core, row, yl * 4 + xx]).astype(jnp.int32)

    def swap(value, axis):
        return lax.ppermute(value, axis, [(0, 1), (1, 0)])

    def across(value, dz, dy, dx):
        perm = [(i, i ^ (dz * 16 + dy * 4 + dx)) for i in range(128)]
        return lax.ppermute(value, ("row", "yl", "x"), perm)

    barrier = lax.optimization_barrier
    share = lax.dynamic_slice(grad_out, (row * 16, (1 - yh) * (hidden // 2)), (16, hidden // 2))
    share, acts_in = barrier((share, acts))
    share = swap(share, "yh")
    weight_far = swap(weight, "core")

    total, send = prepare(acts_in, grad_out)
    total = total + across(send, 1, 0, 1).astype(F32)
    send, share = barrier((total.astype(BF), share))
    total = total + across(send, 2, 0, 3).astype(F32)
    near = product(place, grad_out, weight, weight_far)
    total = total + across(total.astype(BF), 7, 1, 0).astype(F32)
    left, right = total[0], total[1]
    send, near = barrier((left.astype(BF), near))
    left = left + across(send, 0, 2, 0).astype(F32)

    share = jnp.broadcast_to(share[None], (8,) + share.shape)
    far_tokens = lax.all_to_all(share, "row", 0, 0, tiled=True)

    keep, send = stats(place, left, right, acts, grad_out)
    send, far_tokens = barrier((send, far_tokens))
    both = product(place, far_tokens, weight, weight_far, near)
    near_rows, far_rows = core_sum(keep, swap(send, "core"))
    both, near_rows = barrier((both, near_rows))
    far_rows = swap(far_rows, "yh")
    got = lax.all_to_all(both, "x", 0, 0, tiled=True)

    chunks = x_sum(place, got)
    chunks = chunks.reshape(8, -1, chunks.shape[2])
    chunks, far_rows = barrier((chunks, far_rows))
    input_grad = y_sum(lax.all_to_all(chunks, ("yh", "yl"), 0, 0, tiled=True))

    left_stats, right_stats = last_sum(near_rows, far_rows, hidden, width)
    return input_grad, left_stats, right_stats


def solution(mesh):
    split = Mesh(mesh.devices.reshape(2, 2, 8, 4, 4), ("yh", "core", "row", "yl", "x"))
    rep, col = ("yh", "core"), ("yl", "x")
    in_specs = (P(rep, "row"), P(rep, col), P(rep, "row", col))
    out_specs = (P(rep + col, "row"), P(rep + col, "row"), P(rep + ("row",), col))
    return jax.shard_map(body, mesh=split, in_specs=in_specs, out_specs=out_specs, check_vma=False)
```

```python
import functools

import jax
import jax.numpy as jnp
from jax import lax
from jax.experimental import pallas as pl
from jax.experimental.pallas import tpu as pltpu
from jax.sharding import Mesh, PartitionSpec as P

D = 16384
FF = 49152
BLOCK = 1024
TOKENS = 512
NT = (((1,), (1,)), ((), ()))
BF = jnp.bfloat16
F32 = jnp.float32
MB = 1024 * 1024


def params(mb):
    return pltpu.CompilerParams(vmem_limit_bytes=mb * MB)


def cost(flops, moved):
    return pl.CostEstimate(flops=flops, bytes_accessed=moved, transcendentals=0)


def prepare_kernel(acts_ref, grads_ref, sum_ref, send_ref):
    for i, ref in enumerate((grads_ref, acts_ref)):
        data = ref[...]
        value = lax.dot_general(data, data, NT, preferred_element_type=F32)
        sum_ref[i] = value
        send_ref[i] = value.astype(BF)


def prepare(acts, grads):
    tokens = grads.shape[0]
    vmem = pl.BlockSpec(memory_space=pltpu.VMEM)
    return pl.pallas_call(
        prepare_kernel,
        out_shape=(jax.ShapeDtypeStruct((2, tokens, tokens), F32), jax.ShapeDtypeStruct((2, tokens, tokens), BF)),
        in_specs=[vmem, vmem],
        out_specs=[vmem] * 2,
        compiler_params=params(16),
        cost_estimate=cost(2 * tokens * tokens * (grads.shape[1] + acts.shape[1]), 3 * MB),
    )(acts, grads)


def product_kernel(place, near_ref, far_ref, own_lo, own_hi, other_lo, other_hi, out_ref, low, high):
    quarter = own_lo.shape[1]
    half = near_ref.shape[0]

    def piece(core):
        lanes = pl.ds(pl.multiple_of(core * quarter, quarter), quarter)
        return jnp.concatenate([near_ref[:, lanes], far_ref[:, :, lanes].reshape(half, quarter)], axis=0)

    own, other = piece(place[1]), piece(1 - place[1])

    def dot(first, second):
        return lax.dot_general(own, first[...], NT, preferred_element_type=F32) + lax.dot_general(
            other, second[...], NT, preferred_element_type=F32
        )

    low[...] = dot(own_lo, other_lo)
    high[...] = dot(own_hi, other_hi)
    for x in range(4):
        for y in range(8):
            rows = slice((y * 4 + x) * 8, (y * 4 + x) * 8 + 8)
            pair = jnp.concatenate([low[rows, :], high[rows, :]], axis=0).astype(BF)
            out_ref[x, y * 16 : y * 16 + 16, :] = pair


def product(place, near, far, weight, weight_far):
    features, quarter = weight.shape
    half = features // 2
    step = 256
    steps = half // step
    low = pl.BlockSpec((step, quarter), lambda j, place: (j, 0))
    high = pl.BlockSpec((step, quarter), lambda j, place: (j + steps, 0))
    count = near.shape[0]
    return pl.pallas_call(
        product_kernel,
        out_shape=jax.ShapeDtypeStruct((4, count, half), BF),
        grid_spec=pltpu.PrefetchScalarGridSpec(
            num_scalar_prefetch=1,
            grid=(steps,),
            in_specs=[
                pl.BlockSpec((count, 2 * quarter), lambda j, place: (0, place[0])),
                pl.BlockSpec(far.shape, lambda j, place: (0, 0, 0)),
                low,
                high,
                low,
                high,
            ],
            out_specs=pl.BlockSpec((4, count, step), lambda j, place: (0, 0, j)),
            scratch_shapes=[pltpu.VMEM((2 * count, step), F32)] * 2,
        ),
        compiler_params=params(60),
        cost_estimate=cost(8 * count * features * quarter, 8 * MB),
    )(place, near, far, weight, weight, weight_far, weight_far)


def x_sum_kernel(place, got_ref, out_ref):
    rows = out_ref.shape[1]
    for part in range(2):
        value = got_ref[0, part * rows : part * rows + rows, :].astype(F32)
        for i in range(1, got_ref.shape[0]):
            value = value + got_ref[i, part * rows : part * rows + rows, :].astype(F32)
        out_ref[(1 - place[0]) if part else place[0]] = value.astype(BF)


def x_sum(place, got):
    _, rows, width = got.shape
    vmem = pl.BlockSpec(memory_space=pltpu.VMEM)
    return pl.pallas_call(
        x_sum_kernel,
        out_shape=jax.ShapeDtypeStruct((2, rows // 2, width), BF),
        in_specs=[pl.BlockSpec(memory_space=pltpu.SMEM), vmem],
        out_specs=vmem,
        compiler_params=params(16),
        cost_estimate=cost(8 * rows * width, 2 * MB),
    )(place, got)


def y_sum_kernel(got_ref, out_ref):
    value = got_ref[0].astype(F32)
    for i in range(1, got_ref.shape[0]):
        value = value + got_ref[i].astype(F32)
    out_ref[...] = jnp.concatenate([value[:8], value[8:]], axis=1).astype(BF)


def y_sum(got):
    width = got.shape[2]
    return pl.pallas_call(
        y_sum_kernel,
        out_shape=jax.ShapeDtypeStruct((8, 2 * width), BF),
        in_specs=[pl.BlockSpec(memory_space=pltpu.VMEM)],
        out_specs=pl.BlockSpec(memory_space=pltpu.VMEM),
        compiler_params=params(16),
        cost_estimate=cost(128 * width, MB // 2),
    )(got)


def picker(place, offset, share, stride):
    shape = (4 * share, BLOCK)
    row = lax.broadcasted_iota(jnp.int32, shape, 0)
    unit = lax.broadcasted_iota(jnp.int32, shape, 1)
    peer = row // share
    rep = (place[0] ^ (peer & 1)) * 2 + (place[1] ^ (peer >> 1))
    wanted = (rep * stride + offset) * share + (row % share)
    return jnp.where(unit == wanted, 1.0, 0.0).astype(BF)


def stats_kernel(place, total_ref, pair_ref, left2_ref, left3_ref, acts_hbm, grads_hbm, keep_ref, send_ref, acts_ref, grads_ref, sems):
    hidden = grads_ref.shape[1]
    width = acts_ref.shape[1]
    copies = []
    for j in range((hidden + width) // BLOCK):
        source, target, at = (grads_hbm, grads_ref, j) if j < hidden // BLOCK else (acts_hbm, acts_ref, j - hidden // BLOCK)
        lanes = slice(at * BLOCK, (at + 1) * BLOCK)
        copies.append(pltpu.make_async_copy(source.at[:, lanes], target.at[:, lanes], sems.at[j]))
        copies[-1].start()

    def rows(pick, token_kernel, data):
        mix = jnp.dot(token_kernel, data, preferred_element_type=F32).astype(BF)
        picked = lax.dot_general(pick, data, NT, preferred_element_type=F32).astype(BF)
        return jnp.dot(picked, mix, preferred_element_type=F32) * (1.0 / TOKENS)

    right = total_ref[1] + pair_ref[1].astype(F32)
    right = (right / D).astype(BF)
    pick = picker(place, place[2], 32, 8)
    for j in range(hidden // BLOCK):
        lanes = slice(j * BLOCK, (j + 1) * BLOCK)
        copies[j].wait()
        out = rows(pick, right, grads_ref[:, lanes])
        keep_ref[:, lanes] = out[:64]
        send_ref[:, lanes] = out[64:]
    left = total_ref[0] + pair_ref[0].astype(F32) + left2_ref[...].astype(F32) + left3_ref[...].astype(F32)
    left = (left / FF).astype(BF)
    pick = picker(place, place[3], 16, 16)
    for j in range(width // BLOCK):
        copies[hidden // BLOCK + j].wait()
        out = rows(pick, left, acts_ref[:, j * BLOCK : (j + 1) * BLOCK])
        for dy in range(2):
            at = slice(dy * 32 + j * 16, dy * 32 + j * 16 + 16)
            keep_ref[at, hidden:] = out[dy * 16 : dy * 16 + 16]
            send_ref[at, hidden:] = out[32 + dy * 16 : 32 + dy * 16 + 16]


def stats(place, total, pair, left2, left3, acts, grads):
    shape = jax.ShapeDtypeStruct((64, grads.shape[1] + BLOCK), F32)
    vmem = pl.BlockSpec(memory_space=pltpu.VMEM)
    hbm = pl.BlockSpec(memory_space=pltpu.HBM)
    return pl.pallas_call(
        stats_kernel,
        out_shape=(shape, shape),
        in_specs=[pl.BlockSpec(memory_space=pltpu.SMEM)] + [vmem] * 4 + [hbm, hbm],
        out_specs=[vmem, vmem],
        scratch_shapes=[
            pltpu.VMEM(acts.shape, BF),
            pltpu.VMEM(grads.shape, BF),
            pltpu.SemaphoreType.DMA(((acts.shape[1] + grads.shape[1]) // BLOCK,)),
        ],
        compiler_params=params(16),
        cost_estimate=cost(1000 * MB, 5 * MB),
    )(place, total, pair, left2, left3, acts, grads)


def core_sum_kernel(keep_ref, got_ref, near_ref, far_ref):
    half = near_ref.shape[0]
    near_ref[...] = keep_ref[:half] + got_ref[:half]
    far_ref[...] = (keep_ref[half:] + got_ref[half:]).astype(BF)


def core_sum(keep, got):
    rows, width = keep.shape
    vmem = pl.BlockSpec(memory_space=pltpu.VMEM)
    return pl.pallas_call(
        core_sum_kernel,
        out_shape=(
            jax.ShapeDtypeStruct((rows // 2, width), F32),
            jax.ShapeDtypeStruct((rows // 2, width), BF),
        ),
        in_specs=[vmem, vmem],
        out_specs=[vmem, vmem],
        compiler_params=params(16),
        cost_estimate=cost(rows * width, 3 * MB),
    )(keep, got)


def last_sum_kernel(near_ref, far_ref, left_ref, right_ref):
    hidden = right_ref.shape[1]
    right_ref[...] = near_ref[:, :hidden] + far_ref[:, :hidden].astype(F32)
    for j in range(left_ref.shape[1] // BLOCK):
        rows = slice(j * 16, j * 16 + 16)
        left_ref[:, j * BLOCK : (j + 1) * BLOCK] = near_ref[rows, hidden:] + far_ref[rows, hidden:].astype(F32)


def last_sum(near, far, hidden, width):
    vmem = pl.BlockSpec(memory_space=pltpu.VMEM)
    return pl.pallas_call(
        last_sum_kernel,
        out_shape=(
            jax.ShapeDtypeStruct((16, width), F32),
            jax.ShapeDtypeStruct((32, hidden), F32),
        ),
        in_specs=[vmem, vmem],
        out_specs=[vmem, vmem],
        compiler_params=params(16),
        cost_estimate=cost(32 * 4096, 2 * MB),
    )(near, far)


def body(acts, grad_out, weight_slab):
    weight = weight_slab[0]
    width = acts.shape[1]
    hidden = grad_out.shape[1]
    yh, core, row, yl, xx = (lax.axis_index(n) for n in ("yh", "core", "row", "yl", "x"))
    place = jnp.stack([yh, core, row, yl * 4 + xx]).astype(jnp.int32)

    def swap(value, axis):
        return lax.ppermute(value, axis, [(0, 1), (1, 0)])

    def across(value, dz, dy, dx):
        perm = [(i, i ^ (dz * 16 + dy * 4 + dx)) for i in range(128)]
        return lax.ppermute(value, ("row", "yl", "x"), perm)

    barrier = lax.optimization_barrier
    share = lax.dynamic_slice(grad_out, (row * 16, (1 - yh) * (hidden // 2)), (16, hidden // 2))
    share, acts_in = barrier((share, acts))
    share = swap(share, "yh")
    weight_far = swap(weight, "core")

    total, send = prepare(acts_in, grad_out)
    share = jnp.broadcast_to(share[None], (8,) + share.shape)
    send, share = barrier((send, share))
    far_tokens = lax.all_to_all(share, "row", 0, 0, tiled=True)
    parts = [across(send, r, 0, r).astype(F32) for r in (1, 2, 3)]
    total = total + parts[0] + parts[1] + parts[2]
    send = total.astype(BF)
    pair = across(send, 7, 1, 0)
    left2 = across(send[0], 0, 2, 0)

    both = product(place, grad_out, far_tokens, weight, weight_far)
    both, last = barrier((both, send[0]))
    left3 = across(last, 0, 3, 0)
    got = lax.all_to_all(both, "x", 0, 0, tiled=True)

    keep, send = stats(place, total, pair, left2, left3, acts, grad_out)
    back, got = barrier((swap(send, "core"), got))
    near_rows, far_rows = core_sum(keep, back)
    got, near_rows = barrier((got, near_rows))
    far_rows = swap(far_rows, "yh")

    chunks = x_sum(place, got)
    chunks = chunks.reshape(8, -1, chunks.shape[2])
    input_grad = y_sum(lax.all_to_all(chunks, ("yh", "yl"), 0, 0, tiled=True))

    left_stats, right_stats = last_sum(near_rows, far_rows, hidden, width)
    return input_grad, left_stats, right_stats


def solution(mesh):
    split = Mesh(mesh.devices.reshape(2, 2, 8, 4, 4), ("yh", "core", "row", "yl", "x"))
    rep, col = ("yh", "core"), ("yl", "x")
    in_specs = (P(rep, "row"), P(rep, col), P(rep, "row", col))
    out_specs = (P(rep + col, "row"), P(rep + col, "row"), P(rep + ("row",), col))
    return jax.shard_map(body, mesh=split, in_specs=in_specs, out_specs=out_specs, check_vma=False)
```

```python
import functools

import jax
import jax.numpy as jnp
from jax import lax
from jax.experimental import pallas as pl
from jax.experimental.pallas import tpu as pltpu
from jax.sharding import Mesh, PartitionSpec as P

D = 16384
FF = 49152
BLOCK = 1024
TOKENS = 512
NT = (((1,), (1,)), ((), ()))
BF = jnp.bfloat16
F32 = jnp.float32
MB = 1024 * 1024


def params(mb):
    return pltpu.CompilerParams(vmem_limit_bytes=mb * MB)


def cost():
    return pl.CostEstimate(flops=1, bytes_accessed=1, transcendentals=0)


def prepare_kernel(acts_ref, grads_ref, sum_ref, send_ref):
    for i, ref in enumerate((grads_ref, acts_ref)):
        data = ref[...]
        value = lax.dot_general(data, data, NT, preferred_element_type=F32)
        sum_ref[i] = value
        send_ref[i] = value.astype(BF)


def prepare(acts, grads):
    tokens = grads.shape[0]
    vmem = pl.BlockSpec(memory_space=pltpu.VMEM)
    return pl.pallas_call(
        prepare_kernel,
        out_shape=(jax.ShapeDtypeStruct((2, tokens, tokens), F32), jax.ShapeDtypeStruct((2, tokens, tokens), BF)),
        in_specs=[vmem, vmem],
        out_specs=[vmem] * 2,
        compiler_params=params(16),
        cost_estimate=cost(),
    )(acts, grads)


def product_kernel(place, near_ref, far_ref, own_lo, own_hi, other_lo, other_hi, out_ref, low, high):
    quarter = own_lo.shape[1]
    half = near_ref.shape[0]

    def piece(core):
        lanes = pl.ds(pl.multiple_of(core * quarter, quarter), quarter)
        return jnp.concatenate([near_ref[:, lanes], far_ref[:, :, lanes].reshape(half, quarter)], axis=0)

    own, other = piece(place[1]), piece(1 - place[1])

    def dot(first, second):
        return lax.dot_general(own, first[...], NT, preferred_element_type=F32) + lax.dot_general(
            other, second[...], NT, preferred_element_type=F32
        )

    low[...] = dot(own_lo, other_lo)
    high[...] = dot(own_hi, other_hi)
    for x in range(4):
        for y in range(8):
            rows = slice((y * 4 + x) * 8, (y * 4 + x) * 8 + 8)
            pair = jnp.concatenate([low[rows, :], high[rows, :]], axis=0).astype(BF)
            out_ref[x, y * 16 : y * 16 + 16, :] = pair


def product(place, near, far, weight, weight_far):
    features, quarter = weight.shape
    half = features // 2
    step = 256
    steps = half // step
    low = pl.BlockSpec((step, quarter), lambda j, place: (j, 0))
    high = pl.BlockSpec((step, quarter), lambda j, place: (j + steps, 0))
    count = near.shape[0]
    return pl.pallas_call(
        product_kernel,
        out_shape=jax.ShapeDtypeStruct((4, count, half), BF),
        grid_spec=pltpu.PrefetchScalarGridSpec(
            num_scalar_prefetch=1,
            grid=(steps,),
            in_specs=[
                pl.BlockSpec((count, 2 * quarter), lambda j, place: (0, place[0])),
                pl.BlockSpec(far.shape, lambda j, place: (0, 0, 0)),
                low,
                high,
                low,
                high,
            ],
            out_specs=pl.BlockSpec((4, count, step), lambda j, place: (0, 0, j)),
            scratch_shapes=[pltpu.VMEM((2 * count, step), F32)] * 2,
        ),
        compiler_params=params(60),
        cost_estimate=cost(),
    )(place, near, far, weight, weight, weight_far, weight_far)


def x_sum_kernel(place, got_ref, out_ref):
    rows = out_ref.shape[1]
    for part in range(2):
        value = got_ref[0, part * rows : part * rows + rows, :].astype(F32)
        for i in range(1, got_ref.shape[0]):
            value = value + got_ref[i, part * rows : part * rows + rows, :].astype(F32)
        out_ref[(1 - place[0]) if part else place[0]] = value.astype(BF)


def x_sum(place, got):
    _, rows, width = got.shape
    vmem = pl.BlockSpec(memory_space=pltpu.VMEM)
    return pl.pallas_call(
        x_sum_kernel,
        out_shape=jax.ShapeDtypeStruct((2, rows // 2, width), BF),
        in_specs=[pl.BlockSpec(memory_space=pltpu.SMEM), vmem],
        out_specs=vmem,
        compiler_params=params(16),
        cost_estimate=cost(),
    )(place, got)


def y_sum_kernel(got_ref, out_ref):
    value = got_ref[0].astype(F32)
    for i in range(1, got_ref.shape[0]):
        value = value + got_ref[i].astype(F32)
    out_ref[...] = jnp.concatenate([value[:8], value[8:]], axis=1).astype(BF)


def y_sum(got):
    width = got.shape[2]
    return pl.pallas_call(
        y_sum_kernel,
        out_shape=jax.ShapeDtypeStruct((8, 2 * width), BF),
        in_specs=[pl.BlockSpec(memory_space=pltpu.VMEM)],
        out_specs=pl.BlockSpec(memory_space=pltpu.VMEM),
        compiler_params=params(16),
        cost_estimate=cost(),
    )(got)


def picker(place, offset, share, stride):
    shape = (4 * share, BLOCK)
    row = lax.broadcasted_iota(jnp.int32, shape, 0)
    unit = lax.broadcasted_iota(jnp.int32, shape, 1)
    peer = row // share
    rep = (place[0] ^ (peer & 1)) * 2 + (place[1] ^ (peer >> 1))
    wanted = (rep * stride + offset) * share + (row % share)
    return jnp.where(unit == wanted, 1.0, 0.0).astype(BF)


def stats_kernel(place, left_ref, right_ref, acts_hbm, grads_hbm, keep_ref, send_ref, acts_ref, grads_ref, sems):
    hidden = grads_ref.shape[1]
    width = acts_ref.shape[1]
    copies = []
    for j in range((hidden + width) // BLOCK):
        source, target, at = (grads_hbm, grads_ref, j) if j < hidden // BLOCK else (acts_hbm, acts_ref, j - hidden // BLOCK)
        lanes = slice(at * BLOCK, (at + 1) * BLOCK)
        copies.append(pltpu.make_async_copy(source.at[:, lanes], target.at[:, lanes], sems.at[j]))
        copies[-1].start()

    def rows(pick, token_kernel, data):
        mix = jnp.dot(token_kernel, data, preferred_element_type=F32).astype(BF)
        picked = lax.dot_general(pick, data, NT, preferred_element_type=F32).astype(BF)
        return jnp.dot(picked, mix, preferred_element_type=F32) * (1.0 / TOKENS)

    right = (right_ref[...] / D).astype(BF)
    pick = picker(place, place[2], 32, 8)
    for j in range(hidden // BLOCK):
        lanes = slice(j * BLOCK, (j + 1) * BLOCK)
        copies[j].wait()
        out = rows(pick, right, grads_ref[:, lanes])
        keep_ref[:, lanes] = out[:64]
        send_ref[:, lanes] = out[64:]
    left = (left_ref[...] / FF).astype(BF)
    pick = picker(place, place[3], 16, 16)
    for j in range(width // BLOCK):
        copies[hidden // BLOCK + j].wait()
        out = rows(pick, left, acts_ref[:, j * BLOCK : (j + 1) * BLOCK])
        for dy in range(2):
            at = slice(dy * 32 + j * 16, dy * 32 + j * 16 + 16)
            keep_ref[at, hidden:] = out[dy * 16 : dy * 16 + 16]
            send_ref[at, hidden:] = out[32 + dy * 16 : 32 + dy * 16 + 16]


def stats(place, left, right, acts, grads):
    shape = jax.ShapeDtypeStruct((64, grads.shape[1] + BLOCK), F32)
    vmem = pl.BlockSpec(memory_space=pltpu.VMEM)
    hbm = pl.BlockSpec(memory_space=pltpu.HBM)
    return pl.pallas_call(
        stats_kernel,
        out_shape=(shape, shape),
        in_specs=[pl.BlockSpec(memory_space=pltpu.SMEM), vmem, vmem, hbm, hbm],
        out_specs=[vmem, vmem],
        scratch_shapes=[
            pltpu.VMEM(acts.shape, BF),
            pltpu.VMEM(grads.shape, BF),
            pltpu.SemaphoreType.DMA(((acts.shape[1] + grads.shape[1]) // BLOCK,)),
        ],
        compiler_params=params(16),
        cost_estimate=cost(),
    )(place, left, right, acts, grads)


def core_sum_kernel(keep_ref, got_ref, near_ref, far_ref):
    half = near_ref.shape[0]
    near_ref[...] = keep_ref[:half] + got_ref[:half]
    far_ref[...] = (keep_ref[half:] + got_ref[half:]).astype(BF)


def core_sum(keep, got):
    rows, width = keep.shape
    vmem = pl.BlockSpec(memory_space=pltpu.VMEM)
    return pl.pallas_call(
        core_sum_kernel,
        out_shape=(
            jax.ShapeDtypeStruct((rows // 2, width), F32),
            jax.ShapeDtypeStruct((rows // 2, width), BF),
        ),
        in_specs=[vmem, vmem],
        out_specs=[vmem, vmem],
        compiler_params=params(16),
        cost_estimate=cost(),
    )(keep, got)


def last_sum_kernel(near_ref, far_ref, left_ref, right_ref):
    hidden = right_ref.shape[1]
    right_ref[...] = near_ref[:, :hidden] + far_ref[:, :hidden].astype(F32)
    for j in range(left_ref.shape[1] // BLOCK):
        rows = slice(j * 16, j * 16 + 16)
        left_ref[:, j * BLOCK : (j + 1) * BLOCK] = near_ref[rows, hidden:] + far_ref[rows, hidden:].astype(F32)


def last_sum(near, far, hidden, width):
    vmem = pl.BlockSpec(memory_space=pltpu.VMEM)
    return pl.pallas_call(
        last_sum_kernel,
        out_shape=(
            jax.ShapeDtypeStruct((16, width), F32),
            jax.ShapeDtypeStruct((32, hidden), F32),
        ),
        in_specs=[vmem, vmem],
        out_specs=[vmem, vmem],
        compiler_params=params(16),
        cost_estimate=cost(),
    )(near, far)


def body(acts, grad_out, weight_slab):
    weight = weight_slab[0]
    width = acts.shape[1]
    hidden = grad_out.shape[1]
    yh, core, row, yl, xx = (lax.axis_index(n) for n in ("yh", "core", "row", "yl", "x"))
    place = jnp.stack([yh, core, row, yl * 4 + xx]).astype(jnp.int32)

    def swap(value, axis):
        return lax.ppermute(value, axis, [(0, 1), (1, 0)])

    def across(value, dz, dy, dx):
        perm = [(i, i ^ (dz * 16 + dy * 4 + dx)) for i in range(128)]
        return lax.ppermute(value, ("row", "yl", "x"), perm)

    barrier = lax.optimization_barrier
    share = lax.dynamic_slice(grad_out, (row * 16, (1 - yh) * (hidden // 2)), (16, hidden // 2))
    share, acts_in = barrier((share, acts))
    share = swap(share, "yh")
    weight_far = swap(weight, "core")

    total, send = prepare(acts_in, grad_out)
    total = total + across(send, 1, 0, 1).astype(F32)
    send, share = barrier((total.astype(BF), share))
    total = total + across(send, 2, 0, 3).astype(F32)
    total = total + across(total.astype(BF), 7, 1, 0).astype(F32)
    left, right = total[0], total[1]
    share = jnp.broadcast_to(share[None], (8,) + share.shape)
    send, share = barrier((left.astype(BF), share))
    far_tokens = lax.all_to_all(share, "row", 0, 0, tiled=True)
    left = left + across(send, 0, 2, 0).astype(F32)

    keep, send = stats(place, left, right, acts, grad_out)
    far_tokens, send = barrier((far_tokens, send))
    both = product(place, grad_out, far_tokens, weight, weight_far)
    both, send = barrier((both, send))
    got = lax.all_to_all(both, "x", 0, 0, tiled=True)
    near_rows, far_rows = core_sum(keep, swap(send, "core"))
    got, near_rows = barrier((got, near_rows))
    far_rows = swap(far_rows, "yh")

    chunks = x_sum(place, got)
    chunks = chunks.reshape(8, -1, chunks.shape[2])
    chunks, far_rows = barrier((chunks, far_rows))
    input_grad = y_sum(lax.all_to_all(chunks, ("yh", "yl"), 0, 0, tiled=True))

    left_stats, right_stats = last_sum(near_rows, far_rows, hidden, width)
    return input_grad, left_stats, right_stats


def solution(mesh):
    split = Mesh(mesh.devices.reshape(2, 2, 8, 4, 4), ("yh", "core", "row", "yl", "x"))
    rep, col = ("yh", "core"), ("yl", "x")
    in_specs = (P(rep, "row"), P(rep, col), P(rep, "row", col))
    out_specs = (P(rep + col, "row"), P(rep + col, "row"), P(rep + ("row",), col))
    return jax.shard_map(body, mesh=split, in_specs=in_specs, out_specs=out_specs, check_vma=False)
```

```python
import functools

import jax
import jax.numpy as jnp
from jax import lax
from jax.experimental import pallas as pl
from jax.experimental.pallas import tpu as pltpu
from jax.sharding import Mesh, PartitionSpec as P

D = 16384
FF = 49152
BLOCK = 1024
TOKENS = 512
NT = (((1,), (1,)), ((), ()))
BF = jnp.bfloat16
F32 = jnp.float32
MB = 1024 * 1024


def params(mb):
    return pltpu.CompilerParams(vmem_limit_bytes=mb * MB)


def cost():
    return pl.CostEstimate(flops=1, bytes_accessed=1, transcendentals=0)


def prepare_kernel(acts_ref, grads_ref, sum_ref, send_ref):
    for i, ref in enumerate((grads_ref, acts_ref)):
        data = ref[...]
        value = lax.dot_general(data, data, NT, preferred_element_type=F32)
        sum_ref[i] = value
        send_ref[i] = value.astype(BF)


def prepare(acts, grads):
    tokens = grads.shape[0]
    vmem = pl.BlockSpec(memory_space=pltpu.VMEM)
    return pl.pallas_call(
        prepare_kernel,
        out_shape=(jax.ShapeDtypeStruct((2, tokens, tokens), F32), jax.ShapeDtypeStruct((2, tokens, tokens), BF)),
        in_specs=[vmem, vmem],
        out_specs=[vmem] * 2,
        compiler_params=params(16),
        cost_estimate=cost(),
    )(acts, grads)


def product_kernel(place, near_ref, far_ref, own_lo, own_hi, other_lo, other_hi, out_ref, low, high):
    quarter = own_lo.shape[1]
    half = near_ref.shape[0]

    def piece(core):
        lanes = pl.ds(pl.multiple_of(core * quarter, quarter), quarter)
        return jnp.concatenate([near_ref[:, lanes], far_ref[:, :, lanes].reshape(half, quarter)], axis=0)

    own, other = piece(place[1]), piece(1 - place[1])

    def dot(first, second):
        return lax.dot_general(own, first[...], NT, preferred_element_type=F32) + lax.dot_general(
            other, second[...], NT, preferred_element_type=F32
        )

    low[...] = dot(own_lo, other_lo)
    high[...] = dot(own_hi, other_hi)
    for x in range(4):
        for y in range(8):
            rows = slice((y * 4 + x) * 8, (y * 4 + x) * 8 + 8)
            pair = jnp.concatenate([low[rows, :], high[rows, :]], axis=0).astype(BF)
            out_ref[x, y * 16 : y * 16 + 16, :] = pair


def product(place, near, far, weight, weight_far):
    features, quarter = weight.shape
    half = features // 2
    step = 256
    steps = half // step
    low = pl.BlockSpec((step, quarter), lambda j, place: (j, 0))
    high = pl.BlockSpec((step, quarter), lambda j, place: (j + steps, 0))
    count = near.shape[0]
    return pl.pallas_call(
        product_kernel,
        out_shape=jax.ShapeDtypeStruct((4, count, half), BF),
        grid_spec=pltpu.PrefetchScalarGridSpec(
            num_scalar_prefetch=1,
            grid=(steps,),
            in_specs=[
                pl.BlockSpec((count, 2 * quarter), lambda j, place: (0, place[0])),
                pl.BlockSpec(far.shape, lambda j, place: (0, 0, 0)),
                low,
                high,
                low,
                high,
            ],
            out_specs=pl.BlockSpec((4, count, step), lambda j, place: (0, 0, j)),
            scratch_shapes=[pltpu.VMEM((2 * count, step), F32)] * 2,
        ),
        compiler_params=params(60),
        cost_estimate=cost(),
    )(place, near, far, weight, weight, weight_far, weight_far)


def x_sum_kernel(place, got_ref, out_ref):
    rows = out_ref.shape[1]
    for part in range(2):
        value = got_ref[0, part * rows : part * rows + rows, :].astype(F32)
        for i in range(1, got_ref.shape[0]):
            value = value + got_ref[i, part * rows : part * rows + rows, :].astype(F32)
        out_ref[(1 - place[0]) if part else place[0]] = value.astype(BF)


def x_sum(place, got):
    _, rows, width = got.shape
    vmem = pl.BlockSpec(memory_space=pltpu.VMEM)
    return pl.pallas_call(
        x_sum_kernel,
        out_shape=jax.ShapeDtypeStruct((2, rows // 2, width), BF),
        in_specs=[pl.BlockSpec(memory_space=pltpu.SMEM), vmem],
        out_specs=vmem,
        compiler_params=params(16),
        cost_estimate=cost(),
    )(place, got)


def y_sum_kernel(got_ref, out_ref):
    value = got_ref[0].astype(F32)
    for i in range(1, got_ref.shape[0]):
        value = value + got_ref[i].astype(F32)
    out_ref[...] = jnp.concatenate([value[:8], value[8:]], axis=1).astype(BF)


def y_sum(got):
    width = got.shape[2]
    return pl.pallas_call(
        y_sum_kernel,
        out_shape=jax.ShapeDtypeStruct((8, 2 * width), BF),
        in_specs=[pl.BlockSpec(memory_space=pltpu.VMEM)],
        out_specs=pl.BlockSpec(memory_space=pltpu.VMEM),
        compiler_params=params(16),
        cost_estimate=cost(),
    )(got)


def picker(place, offset, share, stride):
    shape = (4 * share, BLOCK)
    row = lax.broadcasted_iota(jnp.int32, shape, 0)
    unit = lax.broadcasted_iota(jnp.int32, shape, 1)
    peer = row // share
    rep = (place[0] ^ (peer & 1)) * 2 + (place[1] ^ (peer >> 1))
    wanted = (rep * stride + offset) * share + (row % share)
    return jnp.where(unit == wanted, 1.0, 0.0).astype(BF)


def stats_kernel(place, left_ref, right_ref, acts_hbm, grads_hbm, keep_ref, send_ref, acts_ref, grads_ref, sems):
    hidden = grads_ref.shape[1]
    width = acts_ref.shape[1]
    copies = []
    for j in range((hidden + width) // BLOCK):
        source, target, at = (grads_hbm, grads_ref, j) if j < hidden // BLOCK else (acts_hbm, acts_ref, j - hidden // BLOCK)
        lanes = slice(at * BLOCK, (at + 1) * BLOCK)
        copies.append(pltpu.make_async_copy(source.at[:, lanes], target.at[:, lanes], sems.at[j]))
        copies[-1].start()

    def rows(pick, token_kernel, data):
        mix = jnp.dot(token_kernel, data, preferred_element_type=F32).astype(BF)
        picked = lax.dot_general(pick, data, NT, preferred_element_type=F32).astype(BF)
        return jnp.dot(picked, mix, preferred_element_type=F32) * (1.0 / TOKENS)

    right = (right_ref[...] / D).astype(BF)
    pick = picker(place, place[2], 32, 8)
    for j in range(hidden // BLOCK):
        lanes = slice(j * BLOCK, (j + 1) * BLOCK)
        copies[j].wait()
        out = rows(pick, right, grads_ref[:, lanes])
        keep_ref[:, lanes] = out[:64]
        send_ref[:, lanes] = out[64:]
    left = (left_ref[...] / FF).astype(BF)
    pick = picker(place, place[3], 16, 16)
    for j in range(width // BLOCK):
        copies[hidden // BLOCK + j].wait()
        out = rows(pick, left, acts_ref[:, j * BLOCK : (j + 1) * BLOCK])
        for dy in range(2):
            at = slice(dy * 32 + j * 16, dy * 32 + j * 16 + 16)
            keep_ref[at, hidden:] = out[dy * 16 : dy * 16 + 16]
            send_ref[at, hidden:] = out[32 + dy * 16 : 32 + dy * 16 + 16]


def stats(place, left, right, acts, grads):
    shape = jax.ShapeDtypeStruct((64, grads.shape[1] + BLOCK), F32)
    vmem = pl.BlockSpec(memory_space=pltpu.VMEM)
    hbm = pl.BlockSpec(memory_space=pltpu.HBM)
    return pl.pallas_call(
        stats_kernel,
        out_shape=(shape, shape),
        in_specs=[pl.BlockSpec(memory_space=pltpu.SMEM), vmem, vmem, hbm, hbm],
        out_specs=[vmem, vmem],
        scratch_shapes=[
            pltpu.VMEM(acts.shape, BF),
            pltpu.VMEM(grads.shape, BF),
            pltpu.SemaphoreType.DMA(((acts.shape[1] + grads.shape[1]) // BLOCK,)),
        ],
        compiler_params=params(16),
        cost_estimate=cost(),
    )(place, left, right, acts, grads)


def core_sum_kernel(keep_ref, got_ref, near_ref, far_ref):
    half = near_ref.shape[0]
    near_ref[...] = keep_ref[:half] + got_ref[:half]
    far_ref[...] = (keep_ref[half:] + got_ref[half:]).astype(BF)


def core_sum(keep, got):
    rows, width = keep.shape
    vmem = pl.BlockSpec(memory_space=pltpu.VMEM)
    return pl.pallas_call(
        core_sum_kernel,
        out_shape=(
            jax.ShapeDtypeStruct((rows // 2, width), F32),
            jax.ShapeDtypeStruct((rows // 2, width), BF),
        ),
        in_specs=[vmem, vmem],
        out_specs=[vmem, vmem],
        compiler_params=params(16),
        cost_estimate=cost(),
    )(keep, got)


def last_sum_kernel(near_ref, far_ref, left_ref, right_ref):
    hidden = right_ref.shape[1]
    right_ref[...] = near_ref[:, :hidden] + far_ref[:, :hidden].astype(F32)
    for j in range(left_ref.shape[1] // BLOCK):
        rows = slice(j * 16, j * 16 + 16)
        left_ref[:, j * BLOCK : (j + 1) * BLOCK] = near_ref[rows, hidden:] + far_ref[rows, hidden:].astype(F32)


def last_sum(near, far, hidden, width):
    vmem = pl.BlockSpec(memory_space=pltpu.VMEM)
    return pl.pallas_call(
        last_sum_kernel,
        out_shape=(
            jax.ShapeDtypeStruct((16, width), F32),
            jax.ShapeDtypeStruct((32, hidden), F32),
        ),
        in_specs=[vmem, vmem],
        out_specs=[vmem, vmem],
        compiler_params=params(16),
        cost_estimate=cost(),
    )(near, far)


def body(acts, grad_out, weight_slab):
    weight = weight_slab[0]
    width = acts.shape[1]
    hidden = grad_out.shape[1]
    yh, core, row, yl, xx = (lax.axis_index(n) for n in ("yh", "core", "row", "yl", "x"))
    place = jnp.stack([yh, core, row, yl * 4 + xx]).astype(jnp.int32)

    def swap(value, axis):
        return lax.ppermute(value, axis, [(0, 1), (1, 0)])

    def across(value, dz, dy, dx):
        perm = [(i, i ^ (dz * 16 + dy * 4 + dx)) for i in range(128)]
        return lax.ppermute(value, ("row", "yl", "x"), perm)

    barrier = lax.optimization_barrier
    share = lax.dynamic_slice(grad_out, (row * 16, (1 - yh) * (hidden // 2)), (16, hidden // 2))
    share, acts_in = barrier((share, acts))
    share = swap(share, "yh")
    weight_far = swap(weight, "core")

    total, send = prepare(acts_in, grad_out)
    total = total + across(send, 1, 0, 1).astype(F32)
    total = total + across(total.astype(BF), 2, 0, 3).astype(F32)
    total = total + across(total.astype(BF), 7, 1, 0).astype(F32)
    left, right = total[0], total[1]
    share = jnp.broadcast_to(share[None], (8,) + share.shape)
    send, share = barrier((left.astype(BF), share))
    far_tokens = lax.all_to_all(share, "row", 0, 0, tiled=True)
    left = left + across(send, 0, 2, 0).astype(F32)

    keep, send = stats(place, left, right, acts, grad_out)
    far_tokens, send = barrier((far_tokens, send))
    both = product(place, grad_out, far_tokens, weight, weight_far)
    both, send = barrier((both, send))
    got = lax.all_to_all(both, "x", 0, 0, tiled=True)
    near_rows, far_rows = core_sum(keep, swap(send, "core"))
    got, near_rows = barrier((got, near_rows))
    far_rows = swap(far_rows, "yh")

    chunks = x_sum(place, got)
    chunks = chunks.reshape(8, -1, chunks.shape[2])
    chunks, far_rows = barrier((chunks, far_rows))
    input_grad = y_sum(lax.all_to_all(chunks, ("yh", "yl"), 0, 0, tiled=True))

    left_stats, right_stats = last_sum(near_rows, far_rows, hidden, width)
    return input_grad, left_stats, right_stats


def solution(mesh):
    split = Mesh(mesh.devices.reshape(2, 2, 8, 4, 4), ("yh", "core", "row", "yl", "x"))
    rep, col = ("yh", "core"), ("yl", "x")
    in_specs = (P(rep, "row"), P(rep, col), P(rep, "row", col))
    out_specs = (P(rep + col, "row"), P(rep + col, "row"), P(rep + ("row",), col))
    return jax.shard_map(body, mesh=split, in_specs=in_specs, out_specs=out_specs, check_vma=False)
```

```python
import functools

import jax
import jax.numpy as jnp
from jax import lax
from jax.experimental import pallas as pl
from jax.experimental.pallas import tpu as pltpu
from jax.sharding import Mesh, PartitionSpec as P

D = 16384
FF = 49152
BLOCK = 1024
TOKENS = 512
NT = (((1,), (1,)), ((), ()))
BF = jnp.bfloat16
F32 = jnp.float32
MB = 1024 * 1024


def params(mb):
    return pltpu.CompilerParams(vmem_limit_bytes=mb * MB)


def cost():
    return pl.CostEstimate(flops=1, bytes_accessed=1, transcendentals=0)


def prepare_kernel(acts_ref, grads_ref, sum_ref, send_ref):
    for i, ref in enumerate((grads_ref, acts_ref)):
        data = ref[...]
        value = lax.dot_general(data, data, NT, preferred_element_type=F32)
        sum_ref[i] = value
        send_ref[i] = value.astype(BF)


def prepare(acts, grads):
    tokens = grads.shape[0]
    vmem = pl.BlockSpec(memory_space=pltpu.VMEM)
    return pl.pallas_call(
        prepare_kernel,
        out_shape=(jax.ShapeDtypeStruct((2, tokens, tokens), F32), jax.ShapeDtypeStruct((2, tokens, tokens), BF)),
        in_specs=[vmem, vmem],
        out_specs=[vmem] * 2,
        compiler_params=params(16),
        cost_estimate=cost(),
    )(acts, grads)


def product_kernel(place, near_ref, far_ref, own_lo, own_hi, other_lo, other_hi, out_ref, low, high):
    quarter = own_lo.shape[1]
    half = near_ref.shape[0]

    def piece(core):
        lanes = pl.ds(pl.multiple_of(core * quarter, quarter), quarter)
        return jnp.concatenate([near_ref[:, lanes], far_ref[:, :, lanes].reshape(half, quarter)], axis=0)

    own, other = piece(place[1]), piece(1 - place[1])

    def dot(first, second):
        return lax.dot_general(own, first[...], NT, preferred_element_type=F32) + lax.dot_general(
            other, second[...], NT, preferred_element_type=F32
        )

    low[...] = dot(own_lo, other_lo)
    high[...] = dot(own_hi, other_hi)
    for x in range(4):
        for y in range(8):
            rows = slice((y * 4 + x) * 8, (y * 4 + x) * 8 + 8)
            pair = jnp.concatenate([low[rows, :], high[rows, :]], axis=0).astype(BF)
            out_ref[x, y * 16 : y * 16 + 16, :] = pair


def product(place, near, far, weight, weight_far):
    features, quarter = weight.shape
    half = features // 2
    step = 256
    steps = half // step
    low = pl.BlockSpec((step, quarter), lambda j, place: (j, 0))
    high = pl.BlockSpec((step, quarter), lambda j, place: (j + steps, 0))
    count = near.shape[0]
    return pl.pallas_call(
        product_kernel,
        out_shape=jax.ShapeDtypeStruct((4, count, half), BF),
        grid_spec=pltpu.PrefetchScalarGridSpec(
            num_scalar_prefetch=1,
            grid=(steps,),
            in_specs=[
                pl.BlockSpec((count, 2 * quarter), lambda j, place: (0, place[0])),
                pl.BlockSpec(far.shape, lambda j, place: (0, 0, 0)),
                low,
                high,
                low,
                high,
            ],
            out_specs=pl.BlockSpec((4, count, step), lambda j, place: (0, 0, j)),
            scratch_shapes=[pltpu.VMEM((2 * count, step), F32)] * 2,
        ),
        compiler_params=params(60),
        cost_estimate=cost(),
    )(place, near, far, weight, weight, weight_far, weight_far)


def x_sum_kernel(place, got_ref, out_ref):
    rows = out_ref.shape[1]
    for part in range(2):
        value = got_ref[0, part * rows : part * rows + rows, :].astype(F32)
        for i in range(1, got_ref.shape[0]):
            value = value + got_ref[i, part * rows : part * rows + rows, :].astype(F32)
        out_ref[(1 - place[0]) if part else place[0]] = value.astype(BF)


def x_sum(place, got):
    _, rows, width = got.shape
    vmem = pl.BlockSpec(memory_space=pltpu.VMEM)
    return pl.pallas_call(
        x_sum_kernel,
        out_shape=jax.ShapeDtypeStruct((2, rows // 2, width), BF),
        in_specs=[pl.BlockSpec(memory_space=pltpu.SMEM), vmem],
        out_specs=vmem,
        compiler_params=params(16),
        cost_estimate=cost(),
    )(place, got)


def y_sum_kernel(got_ref, out_ref):
    value = got_ref[0].astype(F32)
    for i in range(1, got_ref.shape[0]):
        value = value + got_ref[i].astype(F32)
    out_ref[...] = jnp.concatenate([value[:8], value[8:]], axis=1).astype(BF)


def y_sum(got):
    width = got.shape[2]
    return pl.pallas_call(
        y_sum_kernel,
        out_shape=jax.ShapeDtypeStruct((8, 2 * width), BF),
        in_specs=[pl.BlockSpec(memory_space=pltpu.VMEM)],
        out_specs=pl.BlockSpec(memory_space=pltpu.VMEM),
        compiler_params=params(16),
        cost_estimate=cost(),
    )(got)


def picker(place, offset, share, stride):
    shape = (4 * share, BLOCK)
    row = lax.broadcasted_iota(jnp.int32, shape, 0)
    unit = lax.broadcasted_iota(jnp.int32, shape, 1)
    peer = row // share
    rep = (place[0] ^ (peer & 1)) * 2 + (place[1] ^ (peer >> 1))
    wanted = (rep * stride + offset) * share + (row % share)
    return jnp.where(unit == wanted, 1.0, 0.0).astype(BF)


def stats_kernel(place, total_ref, pair_ref, left2_ref, left3_ref, acts_hbm, grads_hbm, keep_ref, send_ref, acts_ref, grads_ref, sems):
    hidden = grads_ref.shape[1]
    width = acts_ref.shape[1]
    copies = []
    for j in range((hidden + width) // BLOCK):
        source, target, at = (grads_hbm, grads_ref, j) if j < hidden // BLOCK else (acts_hbm, acts_ref, j - hidden // BLOCK)
        lanes = slice(at * BLOCK, (at + 1) * BLOCK)
        copies.append(pltpu.make_async_copy(source.at[:, lanes], target.at[:, lanes], sems.at[j]))
        copies[-1].start()

    def rows(pick, token_kernel, data):
        mix = jnp.dot(token_kernel, data, preferred_element_type=F32).astype(BF)
        picked = lax.dot_general(pick, data, NT, preferred_element_type=F32).astype(BF)
        return jnp.dot(picked, mix, preferred_element_type=F32) * (1.0 / TOKENS)

    right = total_ref[1] + pair_ref[1].astype(F32)
    right = (right / D).astype(BF)
    pick = picker(place, place[2], 32, 8)
    for j in range(hidden // BLOCK):
        lanes = slice(j * BLOCK, (j + 1) * BLOCK)
        copies[j].wait()
        out = rows(pick, right, grads_ref[:, lanes])
        keep_ref[:, lanes] = out[:64]
        send_ref[:, lanes] = out[64:]
    left = total_ref[0] + pair_ref[0].astype(F32) + left2_ref[...].astype(F32) + left3_ref[...].astype(F32)
    left = (left / FF).astype(BF)
    pick = picker(place, place[3], 16, 16)
    for j in range(width // BLOCK):
        copies[hidden // BLOCK + j].wait()
        out = rows(pick, left, acts_ref[:, j * BLOCK : (j + 1) * BLOCK])
        for dy in range(2):
            at = slice(dy * 32 + j * 16, dy * 32 + j * 16 + 16)
            keep_ref[at, hidden:] = out[dy * 16 : dy * 16 + 16]
            send_ref[at, hidden:] = out[32 + dy * 16 : 32 + dy * 16 + 16]


def stats(place, total, pair, left2, left3, acts, grads):
    shape = jax.ShapeDtypeStruct((64, grads.shape[1] + BLOCK), F32)
    vmem = pl.BlockSpec(memory_space=pltpu.VMEM)
    hbm = pl.BlockSpec(memory_space=pltpu.HBM)
    return pl.pallas_call(
        stats_kernel,
        out_shape=(shape, shape),
        in_specs=[pl.BlockSpec(memory_space=pltpu.SMEM)] + [vmem] * 4 + [hbm, hbm],
        out_specs=[vmem, vmem],
        scratch_shapes=[
            pltpu.VMEM(acts.shape, BF),
            pltpu.VMEM(grads.shape, BF),
            pltpu.SemaphoreType.DMA(((acts.shape[1] + grads.shape[1]) // BLOCK,)),
        ],
        compiler_params=params(16),
        cost_estimate=cost(),
    )(place, total, pair, left2, left3, acts, grads)


def core_sum_kernel(keep_ref, got_ref, near_ref, far_ref):
    half = near_ref.shape[0]
    near_ref[...] = keep_ref[:half] + got_ref[:half]
    far_ref[...] = (keep_ref[half:] + got_ref[half:]).astype(BF)


def core_sum(keep, got):
    rows, width = keep.shape
    vmem = pl.BlockSpec(memory_space=pltpu.VMEM)
    return pl.pallas_call(
        core_sum_kernel,
        out_shape=(
            jax.ShapeDtypeStruct((rows // 2, width), F32),
            jax.ShapeDtypeStruct((rows // 2, width), BF),
        ),
        in_specs=[vmem, vmem],
        out_specs=[vmem, vmem],
        compiler_params=params(16),
        cost_estimate=cost(),
    )(keep, got)


def last_sum_kernel(near_ref, far_ref, left_ref, right_ref):
    hidden = right_ref.shape[1]
    right_ref[...] = near_ref[:, :hidden] + far_ref[:, :hidden].astype(F32)
    for j in range(left_ref.shape[1] // BLOCK):
        rows = slice(j * 16, j * 16 + 16)
        left_ref[:, j * BLOCK : (j + 1) * BLOCK] = near_ref[rows, hidden:] + far_ref[rows, hidden:].astype(F32)


def last_sum(near, far, hidden, width):
    vmem = pl.BlockSpec(memory_space=pltpu.VMEM)
    return pl.pallas_call(
        last_sum_kernel,
        out_shape=(
            jax.ShapeDtypeStruct((16, width), F32),
            jax.ShapeDtypeStruct((32, hidden), F32),
        ),
        in_specs=[vmem, vmem],
        out_specs=[vmem, vmem],
        compiler_params=params(16),
        cost_estimate=cost(),
    )(near, far)


def body(acts, grad_out, weight_slab):
    weight = weight_slab[0]
    width = acts.shape[1]
    hidden = grad_out.shape[1]
    yh, core, row, yl, xx = (lax.axis_index(n) for n in ("yh", "core", "row", "yl", "x"))
    place = jnp.stack([yh, core, row, yl * 4 + xx]).astype(jnp.int32)

    def swap(value, axis):
        return lax.ppermute(value, axis, [(0, 1), (1, 0)])

    def across(value, dz, dy, dx):
        perm = [(i, i ^ (dz * 16 + dy * 4 + dx)) for i in range(128)]
        return lax.ppermute(value, ("row", "yl", "x"), perm)

    barrier = lax.optimization_barrier
    share = lax.dynamic_slice(grad_out, (row * 16, (1 - yh) * (hidden // 2)), (16, hidden // 2))
    share, acts_in = barrier((share, acts))
    share = swap(share, "yh")
    weight_far = swap(weight, "core")

    total, send = prepare(acts_in, grad_out)
    total = total + across(send, 1, 0, 1).astype(F32)
    total = total + across(total.astype(BF), 2, 0, 3).astype(F32)
    send = total.astype(BF)
    pair = across(send, 7, 1, 0)
    left2, left3 = across(send[0], 0, 2, 0), across(send[0], 0, 3, 0)

    share = jnp.broadcast_to(share[None], (8,) + share.shape)
    far_tokens = lax.all_to_all(share, "row", 0, 0, tiled=True)

    keep, send = stats(place, total, pair, left2, left3, acts, grad_out)
    near_rows, far_rows = core_sum(keep, swap(send, "core"))
    near_rows, near_tokens, far_tokens = barrier((near_rows, grad_out, far_tokens))
    far_rows = swap(far_rows, "yh")
    both = product(place, near_tokens, far_tokens, weight, weight_far)
    got = lax.all_to_all(both, "x", 0, 0, tiled=True)

    chunks = x_sum(place, got)
    chunks = chunks.reshape(8, -1, chunks.shape[2])
    chunks, far_rows = barrier((chunks, far_rows))
    input_grad = y_sum(lax.all_to_all(chunks, ("yh", "yl"), 0, 0, tiled=True))

    left_stats, right_stats = last_sum(near_rows, far_rows, hidden, width)
    return input_grad, left_stats, right_stats


def solution(mesh):
    split = Mesh(mesh.devices.reshape(2, 2, 8, 4, 4), ("yh", "core", "row", "yl", "x"))
    rep, col = ("yh", "core"), ("yl", "x")
    in_specs = (P(rep, "row"), P(rep, col), P(rep, "row", col))
    out_specs = (P(rep + col, "row"), P(rep + col, "row"), P(rep + ("row",), col))
    return jax.shard_map(body, mesh=split, in_specs=in_specs, out_specs=out_specs, check_vma=False)
```

```python
import functools

import jax
import jax.numpy as jnp
from jax import lax
from jax.experimental import pallas as pl
from jax.experimental.pallas import tpu as pltpu
from jax.sharding import Mesh, PartitionSpec as P

D = 16384
FF = 49152
BLOCK = 1024
TOKENS = 512
NT = (((1,), (1,)), ((), ()))
BF = jnp.bfloat16
F32 = jnp.float32
MB = 1024 * 1024


def params(mb):
    return pltpu.CompilerParams(vmem_limit_bytes=mb * MB)


def cost():
    return pl.CostEstimate(flops=1, bytes_accessed=1, transcendentals=0)


def prepare_kernel(acts_ref, grads_ref, sum_ref, send_ref):
    for i, ref in enumerate((grads_ref, acts_ref)):
        data = ref[...]
        value = lax.dot_general(data, data, NT, preferred_element_type=F32)
        sum_ref[i] = value
        send_ref[i] = value.astype(BF)


def prepare(acts, grads):
    tokens = grads.shape[0]
    vmem = pl.BlockSpec(memory_space=pltpu.VMEM)
    return pl.pallas_call(
        prepare_kernel,
        out_shape=(jax.ShapeDtypeStruct((2, tokens, tokens), F32), jax.ShapeDtypeStruct((2, tokens, tokens), BF)),
        in_specs=[vmem, vmem],
        out_specs=[vmem] * 2,
        compiler_params=params(16),
        cost_estimate=cost(),
    )(acts, grads)


def product_kernel(place, near_ref, far_ref, own_lo, own_hi, other_lo, other_hi, out_ref, low, high):
    quarter = own_lo.shape[1]
    half = near_ref.shape[0]

    def piece(core):
        lanes = pl.ds(pl.multiple_of(core * quarter, quarter), quarter)
        return jnp.concatenate([near_ref[:, lanes], far_ref[:, :, lanes].reshape(half, quarter)], axis=0)

    own, other = piece(place[1]), piece(1 - place[1])

    def dot(first, second):
        return lax.dot_general(own, first[...], NT, preferred_element_type=F32) + lax.dot_general(
            other, second[...], NT, preferred_element_type=F32
        )

    low[...] = dot(own_lo, other_lo)
    high[...] = dot(own_hi, other_hi)
    for x in range(4):
        for y in range(8):
            rows = slice((y * 4 + x) * 8, (y * 4 + x) * 8 + 8)
            pair = jnp.concatenate([low[rows, :], high[rows, :]], axis=0).astype(BF)
            out_ref[x, y * 16 : y * 16 + 16, :] = pair


def product(place, near, far, weight, weight_far):
    features, quarter = weight.shape
    half = features // 2
    step = 256
    steps = half // step
    low = pl.BlockSpec((step, quarter), lambda j, place: (j, 0))
    high = pl.BlockSpec((step, quarter), lambda j, place: (j + steps, 0))
    count = near.shape[0]
    return pl.pallas_call(
        product_kernel,
        out_shape=jax.ShapeDtypeStruct((4, count, half), BF),
        grid_spec=pltpu.PrefetchScalarGridSpec(
            num_scalar_prefetch=1,
            grid=(steps,),
            in_specs=[
                pl.BlockSpec((count, 2 * quarter), lambda j, place: (0, place[0])),
                pl.BlockSpec(far.shape, lambda j, place: (0, 0, 0)),
                low,
                high,
                low,
                high,
            ],
            out_specs=pl.BlockSpec((4, count, step), lambda j, place: (0, 0, j)),
            scratch_shapes=[pltpu.VMEM((2 * count, step), F32)] * 2,
        ),
        compiler_params=params(60),
        cost_estimate=cost(),
    )(place, near, far, weight, weight, weight_far, weight_far)


def x_sum_kernel(place, got_ref, out_ref):
    rows = out_ref.shape[1]
    for part in range(2):
        value = got_ref[0, part * rows : part * rows + rows, :].astype(F32)
        for i in range(1, got_ref.shape[0]):
            value = value + got_ref[i, part * rows : part * rows + rows, :].astype(F32)
        out_ref[(1 - place[0]) if part else place[0]] = value.astype(BF)


def x_sum(place, got):
    _, rows, width = got.shape
    vmem = pl.BlockSpec(memory_space=pltpu.VMEM)
    return pl.pallas_call(
        x_sum_kernel,
        out_shape=jax.ShapeDtypeStruct((2, rows // 2, width), BF),
        in_specs=[pl.BlockSpec(memory_space=pltpu.SMEM), vmem],
        out_specs=vmem,
        compiler_params=params(16),
        cost_estimate=cost(),
    )(place, got)


def y_sum_kernel(got_ref, out_ref):
    value = got_ref[0].astype(F32)
    for i in range(1, got_ref.shape[0]):
        value = value + got_ref[i].astype(F32)
    out_ref[...] = jnp.concatenate([value[:8], value[8:]], axis=1).astype(BF)


def y_sum(got):
    width = got.shape[2]
    return pl.pallas_call(
        y_sum_kernel,
        out_shape=jax.ShapeDtypeStruct((8, 2 * width), BF),
        in_specs=[pl.BlockSpec(memory_space=pltpu.VMEM)],
        out_specs=pl.BlockSpec(memory_space=pltpu.VMEM),
        compiler_params=params(16),
        cost_estimate=cost(),
    )(got)


def picker(place, offset, share, stride):
    shape = (4 * share, BLOCK)
    row = lax.broadcasted_iota(jnp.int32, shape, 0)
    unit = lax.broadcasted_iota(jnp.int32, shape, 1)
    peer = row // share
    rep = (place[0] ^ (peer & 1)) * 2 + (place[1] ^ (peer >> 1))
    wanted = (rep * stride + offset) * share + (row % share)
    return jnp.where(unit == wanted, 1.0, 0.0).astype(BF)


def stats_kernel(place, total_ref, pair_ref, left2_ref, left3_ref, acts_hbm, grads_hbm, keep_ref, send_ref, acts_ref, grads_ref, sems):
    hidden = grads_ref.shape[1]
    width = acts_ref.shape[1]
    copies = []
    for j in range((hidden + width) // BLOCK):
        source, target, at = (grads_hbm, grads_ref, j) if j < hidden // BLOCK else (acts_hbm, acts_ref, j - hidden // BLOCK)
        lanes = slice(at * BLOCK, (at + 1) * BLOCK)
        copies.append(pltpu.make_async_copy(source.at[:, lanes], target.at[:, lanes], sems.at[j]))
        copies[-1].start()

    def rows(pick, token_kernel, data):
        mix = jnp.dot(token_kernel, data, preferred_element_type=F32).astype(BF)
        picked = lax.dot_general(pick, data, NT, preferred_element_type=F32).astype(BF)
        return jnp.dot(picked, mix, preferred_element_type=F32) * (1.0 / TOKENS)

    right = total_ref[1] + pair_ref[1].astype(F32)
    right = (right / D).astype(BF)
    pick = picker(place, place[2], 32, 8)
    for j in range(hidden // BLOCK):
        lanes = slice(j * BLOCK, (j + 1) * BLOCK)
        copies[j].wait()
        out = rows(pick, right, grads_ref[:, lanes])
        keep_ref[:, lanes] = out[:64]
        send_ref[:, lanes] = out[64:]
    left = total_ref[0] + pair_ref[0].astype(F32) + left2_ref[...].astype(F32) + left3_ref[...].astype(F32)
    left = (left / FF).astype(BF)
    pick = picker(place, place[3], 16, 16)
    for j in range(width // BLOCK):
        copies[hidden // BLOCK + j].wait()
        out = rows(pick, left, acts_ref[:, j * BLOCK : (j + 1) * BLOCK])
        for dy in range(2):
            at = slice(dy * 32 + j * 16, dy * 32 + j * 16 + 16)
            keep_ref[at, hidden:] = out[dy * 16 : dy * 16 + 16]
            send_ref[at, hidden:] = out[32 + dy * 16 : 32 + dy * 16 + 16]


def stats(place, total, pair, left2, left3, acts, grads):
    shape = jax.ShapeDtypeStruct((64, grads.shape[1] + BLOCK), F32)
    vmem = pl.BlockSpec(memory_space=pltpu.VMEM)
    hbm = pl.BlockSpec(memory_space=pltpu.HBM)
    return pl.pallas_call(
        stats_kernel,
        out_shape=(shape, shape),
        in_specs=[pl.BlockSpec(memory_space=pltpu.SMEM)] + [vmem] * 4 + [hbm, hbm],
        out_specs=[vmem, vmem],
        scratch_shapes=[
            pltpu.VMEM(acts.shape, BF),
            pltpu.VMEM(grads.shape, BF),
            pltpu.SemaphoreType.DMA(((acts.shape[1] + grads.shape[1]) // BLOCK,)),
        ],
        compiler_params=params(16),
        cost_estimate=cost(),
    )(place, total, pair, left2, left3, acts, grads)


def core_sum_kernel(keep_ref, got_ref, near_ref, far_ref):
    half = near_ref.shape[0]
    near_ref[...] = keep_ref[:half] + got_ref[:half]
    far_ref[...] = (keep_ref[half:] + got_ref[half:]).astype(BF)


def core_sum(keep, got):
    rows, width = keep.shape
    vmem = pl.BlockSpec(memory_space=pltpu.VMEM)
    return pl.pallas_call(
        core_sum_kernel,
        out_shape=(
            jax.ShapeDtypeStruct((rows // 2, width), F32),
            jax.ShapeDtypeStruct((rows // 2, width), BF),
        ),
        in_specs=[vmem, vmem],
        out_specs=[vmem, vmem],
        compiler_params=params(16),
        cost_estimate=cost(),
    )(keep, got)


def last_sum_kernel(near_ref, far_ref, left_ref, right_ref):
    hidden = right_ref.shape[1]
    right_ref[...] = near_ref[:, :hidden] + far_ref[:, :hidden].astype(F32)
    for j in range(left_ref.shape[1] // BLOCK):
        rows = slice(j * 16, j * 16 + 16)
        left_ref[:, j * BLOCK : (j + 1) * BLOCK] = near_ref[rows, hidden:] + far_ref[rows, hidden:].astype(F32)


def last_sum(near, far, hidden, width):
    vmem = pl.BlockSpec(memory_space=pltpu.VMEM)
    return pl.pallas_call(
        last_sum_kernel,
        out_shape=(
            jax.ShapeDtypeStruct((16, width), F32),
            jax.ShapeDtypeStruct((32, hidden), F32),
        ),
        in_specs=[vmem, vmem],
        out_specs=[vmem, vmem],
        compiler_params=params(16),
        cost_estimate=cost(),
    )(near, far)


def body(acts, grad_out, weight_slab):
    weight = weight_slab[0]
    width = acts.shape[1]
    hidden = grad_out.shape[1]
    yh, core, row, yl, xx = (lax.axis_index(n) for n in ("yh", "core", "row", "yl", "x"))
    place = jnp.stack([yh, core, row, yl * 4 + xx]).astype(jnp.int32)

    def swap(value, axis):
        return lax.ppermute(value, axis, [(0, 1), (1, 0)])

    def across(value, dz, dy, dx):
        perm = [(i, i ^ (dz * 16 + dy * 4 + dx)) for i in range(128)]
        return lax.ppermute(value, ("row", "yl", "x"), perm)

    barrier = lax.optimization_barrier
    share = lax.dynamic_slice(grad_out, (row * 16, (1 - yh) * (hidden // 2)), (16, hidden // 2))
    share, acts_in = barrier((share, acts))
    share = swap(share, "yh")
    weight_far = swap(weight, "core")

    total, send = prepare(acts_in, grad_out)
    total = total + across(send, 1, 0, 1).astype(F32)
    total = total + across(total.astype(BF), 2, 0, 3).astype(F32)
    share = jnp.broadcast_to(share[None], (8,) + share.shape)
    send, share = barrier((total.astype(BF), share))
    pair = across(send, 7, 1, 0)
    left2, left3 = across(send[0], 0, 2, 0), across(send[0], 0, 3, 0)

    far_tokens = lax.all_to_all(share, "row", 0, 0, tiled=True)

    keep, send = stats(place, total, pair, left2, left3, acts, grad_out)
    send, far_tokens = barrier((send, far_tokens))
    near_rows, far_rows = core_sum(keep, swap(send, "core"))
    near_rows, near_tokens, far_tokens = barrier((near_rows, grad_out, far_tokens))
    far_rows = swap(far_rows, "yh")
    both = product(place, near_tokens, far_tokens, weight, weight_far)
    got = lax.all_to_all(both, "x", 0, 0, tiled=True)

    chunks = x_sum(place, got)
    chunks = chunks.reshape(8, -1, chunks.shape[2])
    chunks, far_rows = barrier((chunks, far_rows))
    input_grad = y_sum(lax.all_to_all(chunks, ("yh", "yl"), 0, 0, tiled=True))

    left_stats, right_stats = last_sum(near_rows, far_rows, hidden, width)
    return input_grad, left_stats, right_stats


def solution(mesh):
    split = Mesh(mesh.devices.reshape(2, 2, 8, 4, 4), ("yh", "core", "row", "yl", "x"))
    rep, col = ("yh", "core"), ("yl", "x")
    in_specs = (P(rep, "row"), P(rep, col), P(rep, "row", col))
    out_specs = (P(rep + col, "row"), P(rep + col, "row"), P(rep + ("row",), col))
    return jax.shard_map(body, mesh=split, in_specs=in_specs, out_specs=out_specs, check_vma=False)
```
